128 devices in a mesh: ens: 4 (over y), cx: 8 (over x, core), cy: 4 (over z).
Axes of the slice: x: 4, y: 4, z: 4, core: 2. Of those that a mesh axis runs over, the one named last changes fastest.
Arguments:
- conformations: float32 [3, 8, 32768, 128], P(None, 'ens', ('cx', 'cy')), may hold values from -2.8 to 2.8
- fill_counts: int32 [8, 32768], P('ens', ('cx', 'cy')), may hold values from 48 to 128
- dest_slots: int32 [8, 32768], P('ens', ('cx', 'cy')), may hold values from 0 to 1535, as said below
- dest_cells: int32 [8, 32768], P('ens', ('cx', 'cy')), may hold values from 0 to 2047
- velocity: float32 [3, 64, 1024], P(None, 'cx', 'cy'), may hold values from -6 to 6
- noise: float32 [3, 8, 49152, 128], P(None, 'ens', ('cx', 'cy')), may hold values from -6 to 6
Outputs:
- new_conformations: float32 [3, 8, 49152, 128], P(None, 'ens', ('cx', 'cy'))
- new_velocity: float32 [3, 64, 1024], P(None, 'cx', 'cy')
The draws below stay inside these ranges and needn't reach their ends.
Inputs may be any that keep to these rules, and one draw needn't show every extreme that they name: `dest_slots`: within one group the blocks of one device take different slots; slot k sends a block to owner k // 48 of the joined cx+cy axes. In every group some owner receives 48 blocks from every device. `fill_counts`: the live dumbbells of a block fill its first slots. `dest_cells`: A cell of the receiving owner, numbered x first over its 8 x 4 x 64 cells.
All inputs are finite; a program needn't handle non-finite values.
Results may differ from the reference program's by a relative error of at most 0.0003.
Values sent between devices are 32-bit elements; how exact they have to be, the bound alone decides.
A program may use at most 128 MiB of HBM per device.

```python
import math
import jax
import jax.numpy as jnp
from jax import lax

SLOTS = 128
DUMB = 64
NZ = 64
CXC = 8
CYC = 4
BLK_DEV = 1024
GROUPS = 8
OWNERS = 32
BLOCKS = 32768
CAP = 48
RBLK = 1536
CELLS = 2048
NX = 64
NY = 16
N_CY = 4


def draw_dest_slots(key, part):
    key = jax.random.fold_in(key, 11)
    hot_key, bias_key, score_key, order_key = jax.random.split(key, 4)
    width_all = OWNERS * CAP
    favoured = jax.random.randint(hot_key, (GROUPS,), 0, OWNERS)
    leaning = jax.random.randint(bias_key, (GROUPS, OWNERS), 0, 2 ** 15)
    owner_ids = jnp.arange(OWNERS, dtype=jnp.int32)
    boosted = jnp.where(owner_ids[None, :] == favoured[:, None], 2 ** 17, leaning)
    scores = jax.random.randint(score_key, (GROUPS, OWNERS, OWNERS, CAP), 0, 2 ** 16)
    scores = (scores + boosted[:, None, :, None]).reshape(GROUPS, OWNERS, width_all)
    keyed_scores = scores * width_all + jnp.arange(width_all, dtype=jnp.int32)
    picked = lax.top_k(keyed_scores, BLK_DEV)[1].astype(jnp.int32)
    shuffle = jax.random.randint(order_key, (GROUPS, OWNERS, BLK_DEV), 0, 2 ** 16) * BLK_DEV + jnp.arange(BLK_DEV, dtype=jnp.int32)
    ordering = jnp.argsort(shuffle, axis=-1)
    return jnp.take_along_axis(picked, ordering, axis=-1).reshape(GROUPS, OWNERS * BLK_DEV)


def set_ends(result, rng, low, top_value):
    spot = [jax.random.randint(jax.random.fold_in(rng, axis), (), 0, length) for axis, length in enumerate(result.shape)]
    longest = result.shape.index(max(result.shape))
    neighbour = spot[:longest] + [(spot[longest] + 1) % result.shape[longest]] + spot[longest + 1:]
    return result.at[tuple(spot)].set(low).at[tuple(neighbour)].set(top_value)


def steps_of(stream_key, dims, pieces, low, largest):
    def one(dim, shards_of):
        heights = jax.random.uniform(jax.random.fold_in(jax.random.fold_in(stream_key, 6), dim), (shards_of,), jnp.float32, low / len(pieces), largest / len(pieces))
        return jnp.repeat(jnp.exp(heights), dims[dim] // shards_of).reshape((-1,) + (1,) * (len(dims) - dim - 1))

    loudness = one(*pieces[0])
    for cut in pieces[1:]:
        loudness = loudness * one(*cut)
    return loudness


def centred(own_key, dims, spread, most, shards=(), kind=jnp.bfloat16):
    values = spread * jax.random.normal(own_key, dims, jnp.float32)
    if shards:
        values = values * steps_of(own_key, dims, shards, -0.22, 0.18)
    return jnp.clip(values, -most, most).astype(kind)


def setup_inputs(seed: int = 0) -> dict:
    key_of = jax.random.split(jax.random.key(seed), 7)
    return {
        "conformations": jnp.clip(jax.random.uniform(key_of[0], (3, GROUPS, BLOCKS, SLOTS), jnp.float32, -2.8, 2.8) * steps_of(key_of[0], (3, GROUPS, BLOCKS, SLOTS), ((1, 4), (2, 32)), -0.4, 0.0), -2.8, 2.8),
        "fill_counts": set_ends(jax.random.randint(key_of[1], (GROUPS, BLOCKS), 3 * SLOTS // 8, SLOTS + 1), jax.random.fold_in(key_of[1], 1), 3 * SLOTS // 8, SLOTS).astype(jnp.int32),
        "dest_slots": draw_dest_slots(jax.random.fold_in(key_of[6], 71), 0),
        "dest_cells": set_ends(jax.random.randint(key_of[3], (GROUPS, BLOCKS), 0, CELLS), jax.random.fold_in(key_of[3], 1), 0, CELLS - 1).astype(jnp.int32),
        "velocity": centred(key_of[4], (3, NX, NY * NZ), 1.0, 6.0, ((1, 8), (2, 4)), jnp.float32),
        "noise": centred(key_of[5], (3, GROUPS, OWNERS * RBLK, SLOTS), 1.0, 6.0, ((1, 4), (2, 32)), jnp.float32),
    }


STRESS_PAIRS = ((0, 0), (1, 1), (2, 2), (0, 1), (0, 2), (1, 2))
PAIR_INDEX = ((0, 3, 4), (3, 1, 5), (4, 5, 2))
TIME_STEP = 0.02
WEISSENBERG = 0.5
EXTENSION = 50.0
VISCOSITY = 1.0

def stencil_parts(padded, depth_cells):
    middle = padded[:, 1:-1, depth_cells:-depth_cells]
    east_side = padded[:, 2:, depth_cells:-depth_cells]
    west_side = padded[:, :-2, depth_cells:-depth_cells]
    north_side = padded[:, 1:-1, 2 * depth_cells:]
    south_side = padded[:, 1:-1, :-2 * depth_cells]
    layer_index = jnp.arange(middle.shape[-1], dtype=jnp.int32) % depth_cells
    blank_edge = jnp.zeros_like(middle[..., :1])
    upper_side = jnp.where(layer_index < depth_cells - 1, jnp.concatenate([middle[..., 1:], blank_edge], axis=-1), 0.0)
    lower_side = jnp.where(layer_index > 0, jnp.concatenate([blank_edge, middle[..., :-1]], axis=-1), 0.0)
    return (middle, east_side, west_side, north_side, south_side, upper_side, lower_side)

def differences(stencil):
    middle, east_side, west_side, north_side, south_side, upper_side, lower_side = stencil
    return (0.5 * (east_side - west_side), 0.5 * (north_side - south_side), 0.5 * (upper_side - lower_side))

def momentum(vel_parts, stress_parts):
    middle, east_side, west_side, north_side, south_side, upper_side, lower_side = vel_parts
    laplace = east_side + west_side + north_side + south_side + upper_side + lower_side - 6.0 * middle
    slopes = differences(stress_parts)
    divergence = jnp.stack([slopes[0][PAIR_INDEX[component][0]] + slopes[1][PAIR_INDEX[component][1]] + slopes[2][PAIR_INDEX[component][2]] for component in range(3)])
    return middle + TIME_STEP * (VISCOSITY * laplace + divergence)

def advance(placed, mask_live, gradient_at, noise_in, normal_count):
    square = lax.optimization_barrier(jnp.sum(placed * placed, axis=0))
    spring = placed / (1.0 - square / EXTENSION)
    stretch = jnp.stack([sum((gradient_at[3 * component + partner][..., None] * placed[partner] for partner in range(3))) for component in range(3)])
    stepped = placed + TIME_STEP * (stretch - spring / (2.0 * WEISSENBERG)) + math.sqrt(TIME_STEP / WEISSENBERG) * noise_in
    updated = jnp.where(mask_live, stepped, 0.0)
    stress = jnp.stack([lax.optimization_barrier(jnp.sum(placed[first_axis] * spring[second_axis], axis=-1)) for first_axis, second_axis in STRESS_PAIRS]) / (WEISSENBERG * normal_count)
    return (updated, stress)

def reference(conformations, fill_counts, dest_slots, dest_cells, velocity, noise):
    vel_parts = stencil_parts(jnp.pad(velocity, ((0, 0), (1, 1), (NZ, NZ))), NZ)
    gradient = jnp.stack(differences(vel_parts), axis=1).reshape(9, -1)
    senders = jnp.arange(BLOCKS, dtype=jnp.int32) // BLK_DEV
    places_count = OWNERS * RBLK
    owner_of = jnp.arange(places_count, dtype=jnp.int32) // RBLK
    row_start = owner_of // N_CY * CXC
    col_start = owner_of % N_CY * (CYC * NZ)
    slots_index = jnp.arange(SLOTS, dtype=jnp.int32)

    def one_group(inputs):
        block_states, block_fill, block_slot, block_cell, group_noise = inputs
        placement = block_slot // CAP * RBLK + senders * CAP + block_slot % CAP
        placed = jnp.zeros((3, places_count, SLOTS), block_states.dtype).at[:, placement].set(block_states)
        fill_at = jnp.zeros((places_count,), jnp.int32).at[placement].set(block_fill)
        cell_at = jnp.zeros((places_count,), jnp.int32).at[placement].set(block_cell)
        mask_live = slots_index[None, :] < fill_at[:, None]
        placed = jnp.where(mask_live, placed, 0.0)
        global_cell = (row_start + cell_at // (CYC * NZ)) * (NY * NZ) + col_start + cell_at % (CYC * NZ)
        updated, stress = advance(placed, mask_live, gradient[:, global_cell], group_noise, DUMB)
        summed = jax.ops.segment_sum(stress.T, global_cell, num_segments=NX * NY * NZ)
        return (updated, summed)
    updated, summed = lax.map(one_group, (jnp.moveaxis(conformations, 1, 0), fill_counts, dest_slots, dest_cells, jnp.moveaxis(noise, 1, 0)))
    stress_field = lax.optimization_barrier(jnp.sum(summed, axis=0)).T.reshape(6, NX, NY * NZ)
    stress_parts = stencil_parts(jnp.pad(stress_field, ((0, 0), (1, 1), (NZ, NZ))), NZ)
    return (jnp.moveaxis(updated, 0, 1), momentum(vel_parts, stress_parts))
```

```python
import functools
import math

import jax
import jax.numpy as jnp
from jax import lax
from jax.experimental import pallas as pl
from jax.experimental.pallas import tpu as pltpu
from jax.sharding import PartitionSpec as P

DUMB = 64
NZ = 64
CAP = 48
TIME_STEP = 0.02
WEISSENBERG = 0.5
EXTENSION = 50.0
VISCOSITY = 1.0

PAIRS = ((0, 0), (1, 1), (2, 2), (0, 1), (0, 2), (1, 2))
ALONG_X = (0, 3, 4)
ALONG_Y = (3, 1, 5)
ALONG_Z = (4, 5, 2)

MESH = pl.DeviceIdType.MESH
F32 = jnp.float32
BF16 = jnp.bfloat16

OFFSETS = (
    (1, 0), (3, 0), (0, 1), (0, 3), (1, 1), (3, 3), (1, 3), (3, 1),
    (2, 0), (0, 2), (2, 1), (1, 2), (2, 3), (3, 2), (2, 2),
)
CODE_X = sum(dx * 4**i for i, (dx, _) in enumerate(OFFSETS))
CODE_Z = sum(dz * 4**i for i, (_, dz) in enumerate(OFFSETS))
HALVES = 2
PART = CAP // HALVES
NT = (((1,), (1,)), ((), ()))


def halves_of(values):
    high = values.astype(BF16)
    return high, (values - high.astype(F32)).astype(BF16)


def stencil(field, west, east, south, north):
    row = lax.broadcasted_iota(jnp.int32, field.shape, 0)
    lane = lax.broadcasted_iota(jnp.int32, field.shape, 1)
    rows, width = field.shape
    east_side = jnp.where(row == rows - 1, pltpu.roll(east, rows - 1, 0), pltpu.roll(field, rows - 1, 0))
    west_side = jnp.where(row == 0, pltpu.roll(west, 1, 0), pltpu.roll(field, 1, 0))
    north_side = jnp.where(
        lane >= width - NZ, pltpu.roll(north, width - NZ, 1), pltpu.roll(field, width - NZ, 1)
    )
    south_side = jnp.where(lane < NZ, pltpu.roll(south, NZ, 1), pltpu.roll(field, NZ, 1))
    return east_side, west_side, north_side, south_side


def along_z(field):
    lane = lax.rem(lax.broadcasted_iota(jnp.int32, field.shape, 1), NZ)
    width = field.shape[1]
    upper = jnp.where(lane < NZ - 1, pltpu.roll(field, width - 1, 1), 0.0)
    lower = jnp.where(lane > 0, pltpu.roll(field, 1, 1), 0.0)
    return upper, lower


def kernel(
    conf_hbm, fill_ref, dest_ref, cell_ref, vel_ref, noise_hbm,
    out_hbm, vout_ref,
    conf, high, low, sendbuf, recv, labsend, labrecv, noise, outbuf,
    vhalo, table, rowbuf, prods, field, sx, sy, shx, shy, dv, base,
    conf_sem, noise_sem, out_sem, ssem, rsem, lssem, lrsem, vs_sem, vr_sem, hs_sem, hr_sem, ds_sem, dr_sem,
):
    ens = lax.axis_index("ens")
    cx = lax.axis_index("cx")
    cy = lax.axis_index("cy")
    my_x = lax.div(cx, 2)
    core = lax.rem(cx, 2)
    n_ens = 4

    for g in range(2):
        pltpu.make_async_copy(conf_hbm.at[:, g], conf.at[:, g], conf_sem.at[g]).start()

    east_id = (ens, lax.rem(cx + 1, 8), cy)
    west_id = (ens, lax.rem(cx + 7, 8), cy)
    north_id = (ens, cx, lax.rem(cy + 1, 4))
    south_id = (ens, cx, lax.rem(cy + 3, 4))

    def chip(dx, dz, r):
        return (ens, lax.rem(my_x + dx, 4) * 2 + lax.rem(core + r, 2), lax.rem(cy + dz, 4))

    barrier = pltpu.get_barrier_semaphore()
    for dx, dz in OFFSETS:
        for r in range(2):
            pl.semaphore_signal(barrier, inc=1, device_id=chip(dx, dz, r), device_id_type=MESH)
    pl.semaphore_signal(barrier, inc=1, device_id=chip(0, 0, 1), device_id_type=MESH)
    for k in range(1, n_ens):
        pl.semaphore_signal(
            barrier, inc=1, device_id=(lax.rem(ens + k, n_ens), cx, cy), device_id_type=MESH
        )

    pltpu.make_async_copy(noise_hbm, noise, noise_sem).start()
    prods[...] = jnp.zeros_like(prods)
    field[...] = jnp.zeros_like(field)
    rowbuf[...] = jnp.zeros_like(rowbuf)
    labsend[...] = jnp.zeros_like(labsend)

    def split(g):
        pltpu.make_async_copy(conf_hbm.at[:, g], conf.at[:, g], conf_sem.at[g]).wait()
        for a in range(3):
            first, second = halves_of(conf[a, g])
            high[g, :, a * 128 : (a + 1) * 128] = first
            low[g, :, a * 128 : (a + 1) * 128] = second

    blocks = conf.shape[2]
    row48 = lax.broadcasted_iota(jnp.int32, (CAP, blocks), 0)
    row16 = lax.broadcasted_iota(jnp.int32, (16, blocks), 0)
    lane128 = lax.broadcasted_iota(jnp.int32, (1, 128), 1)

    split(0)
    pl.semaphore_wait(barrier, 31 + n_ens - 1)

    def vel_copy(slot, target):
        return pltpu.make_async_remote_copy(
            src_ref=vel_ref, dst_ref=vhalo.at[slot], send_sem=vs_sem.at[slot], recv_sem=vr_sem.at[slot],
            device_id=target, device_id_type=MESH,
        )

    halo_targets = (east_id, west_id, north_id, south_id)
    for slot in range(4):
        vel_copy(slot, halo_targets[slot]).start()

    def data_copy(g, i, r, h, target):
        rows = pl.ds(h * PART, PART)
        return pltpu.make_async_remote_copy(
            src_ref=sendbuf.at[g, i, r, :, rows], dst_ref=recv.at[g, i, r, :, rows],
            send_sem=ssem.at[g, i, r], recv_sem=rsem.at[g, i, r],
            device_id=target, device_id_type=MESH,
        )

    def label_copy(g, i, r, target):
        return pltpu.make_async_remote_copy(
            src_ref=labsend.at[g, i, r], dst_ref=labrecv.at[g, i, r],
            send_sem=lssem.at[g, i, r], recv_sem=lrsem.at[g, i, r],
            device_id=target, device_id_type=MESH,
        )

    def pack_batch(q, carry, g):
        code_x, code_z = carry
        dest = dest_ref[g : g + 1, :]
        fill = fill_ref[g : g + 1, :]
        cell = cell_ref[g : g + 1, :]
        pieces = []
        targets = []
        for m in range(4):
            dx, dz = lax.rem(code_x, 4), lax.rem(code_z, 4)
            code_x, code_z = lax.div(code_x, 4), lax.div(code_z, 4)
            for r in range(2):
                target = chip(dx, dz, r)
                owner = target[1] * 4 + target[2]
                targets.append(target)
                pieces.append(jnp.where(dest - owner * CAP == row48, 1.0, 0.0).astype(BF16))
        onehot = jnp.concatenate(pieces, axis=0)
        packed = jnp.dot(onehot, high[g], preferred_element_type=F32) + jnp.dot(
            onehot, low[g], preferred_element_type=F32
        )
        for n in range(8):
            for a in range(3):
                sendbuf[g, 4 * q + n // 2, n % 2, a] = packed[
                    n * CAP : (n + 1) * CAP, a * 128 : (a + 1) * 128
                ]
        labels = jnp.where(
            row16 == 0,
            fill,
            jnp.where(row16 == 1, lax.div(cell, 128), jnp.where(row16 == 2, lax.rem(cell, 128), 0)),
        )
        told = lax.dot_general(labels.astype(F32).astype(BF16), onehot, NT, preferred_element_type=F32)
        fills = told[0:1]
        cells = told[1:2] * 128.0 + told[2:3]
        for n in range(8):
            begin, width = n * CAP, 8 * CAP
            fill_row = pltpu.roll(fills, (width - begin) % width, 1)[:, :128]
            cell_row = pltpu.roll(cells, (width - begin + 64) % width, 1)[:, :128]
            labsend[g, 4 * q + n // 2, n % 2] = jnp.where(
                lane128 < CAP,
                fill_row,
                jnp.where((lane128 >= 64) & (lane128 < 64 + CAP), cell_row, 0.0),
            )

        def send(n):
            i, r = 4 * q + n // 2, n % 2
            label_copy(g, i, r, targets[n]).start()

        def send_part(n, h):
            i, r = 4 * q + n // 2, n % 2
            data_copy(g, i, r, h, targets[n]).start()

        for n in range(6):
            send(n)
        for h in range(HALVES):
            for n in range(6):
                send_part(n, h)

        @pl.when(q < 3)
        def _():
            for n in range(6, 8):
                send(n)
            for h in range(HALVES):
                for n in range(6, 8):
                    send_part(n, h)

        @pl.when(q == 3)
        def _():
            send(7)
            for h in range(HALVES):
                send_part(7, h)
            pltpu.make_async_copy(sendbuf.at[g, 15, 0], recv.at[g, 15, 0], rsem.at[g, 15, 0]).start()
            pltpu.make_async_copy(labsend.at[g, 15, 0], labrecv.at[g, 15, 0], lrsem.at[g, 15, 0]).start()

        return code_x, code_z

    codes = (jnp.int32(CODE_X), jnp.int32(CODE_Z))
    lax.fori_loop(0, 4, functools.partial(pack_batch, g=0), codes)
    split(1)
    lax.fori_loop(0, 4, functools.partial(pack_batch, g=1), codes)

    for slot in range(4):
        vel_copy(slot, halo_targets[slot]).wait()
    inside = (cx > 0, cx < 7, cy > 0, cy < 3)

    def masked(tile, k):
        return jnp.where(inside[k], tile, 0.0)

    for a in range(3):
        f = vel_ref[a]
        e, w, n, s = stencil(f, *(masked(vhalo[k, a], k) for k in range(4)))
        u, d = along_z(f)
        base[a] = f + TIME_STEP * VISCOSITY * (e + w + n + s + u + d - 6.0 * f)
        for b, slope in enumerate((0.5 * (e - w), 0.5 * (n - s), 0.5 * (u - d))):
            first, second = halves_of(jnp.concatenate([slope[:, :128], slope[:, 128:]], axis=0))
            top = (3 * a + b) * 16
            table[top : top + 16] = first
            table[144 + top : 144 + top + 16] = second

    pltpu.make_async_copy(noise_hbm, noise, noise_sem).wait()

    square = lax.broadcasted_iota(jnp.int32, (128, 128), 0)
    row_hi = lax.broadcasted_iota(jnp.int32, (16, 128), 0)
    slot_lane = lax.broadcasted_iota(jnp.int32, (CAP, 128), 1).astype(F32)
    pick_row = lax.broadcasted_iota(jnp.int32, (16, 12 * 128), 0)
    pick_lane = lax.broadcasted_iota(jnp.int32, (16, 12 * 128), 1)
    pick = jnp.where(pick_row == lax.div(pick_lane, 256), 1.0, 0.0).astype(BF16)

    def arrive(j, carry, g):
        code_x, code_z = carry
        own = j == 0
        i = lax.rem(j + 15, 16)
        dx = jnp.where(own, 0, lax.rem(code_x, 4))
        dz = jnp.where(own, 0, lax.rem(code_z, 4))
        code_x = jnp.where(own, code_x, lax.div(code_x, 4))
        code_z = jnp.where(own, code_z, lax.div(code_z, 4))
        for r in range(2):
            pltpu.make_async_copy(labrecv.at[g, i, r], labrecv.at[g, i, r], lrsem.at[g, i, r]).wait()
        lab0, lab1 = labrecv[g, i, 0], labrecv[g, i, 1]
        fills = jnp.where(lane128 < 64, lab0, pltpu.roll(lab1, 64, 1))
        cells = jnp.where(lane128 < 64, pltpu.roll(lab0, 64, 1), lab1).astype(jnp.int32)
        cell_lo = lax.rem(cells, 128)
        cell_hi = lax.div(cells, 128)
        cell_hi = lax.rem(cell_hi, 2) * 8 + lax.div(cell_hi, 2)
        at_lo = jnp.where(square == cell_lo, 1.0, 0.0).astype(BF16)
        at_hi = jnp.where(row_hi == cell_hi, 1.0, 0.0)
        looked = jnp.dot(table[...], at_lo, preferred_element_type=F32)
        looked = looked[:144] + looked[144:]
        for c in range(9):
            rowbuf[c : c + 1] = jnp.sum(looked[16 * c : 16 * c + 16] * at_hi, axis=0, keepdims=True)
        rowbuf[9:10] = fills
        columns = rowbuf[...].T
        for r in range(2):
            pltpu.make_async_copy(recv.at[g, i, r], recv.at[g, i, r], rsem.at[g, i, r]).wait()
        for r in range(2):
            source = (lax.rem(my_x + 4 - dx, 4) * 2 + lax.rem(core + r, 2)) * 4 + lax.rem(cy + 4 - dz, 4)
            rows = pl.ds(pl.multiple_of(source * CAP, CAP), CAP)
            here = columns[r * 64 : r * 64 + CAP]
            live = slot_lane < here[:, 9:10]
            x = [jnp.where(live, recv[g, i, r, a], 0.0) for a in range(3)]
            inverse = 1.0 / (1.0 - (x[0] * x[0] + x[1] * x[1] + x[2] * x[2]) / EXTENSION)
            spring = [x[a] * inverse for a in range(3)]
            for a in range(3):
                stretch = sum(here[:, 3 * a + b : 3 * a + b + 1] * x[b] for b in range(3))
                stepped = (
                    x[a]
                    + TIME_STEP * (stretch - spring[a] / (2.0 * WEISSENBERG))
                    + math.sqrt(TIME_STEP / WEISSENBERG) * noise[a, g, rows]
                )
                outbuf[a, g, rows] = jnp.where(live, stepped, 0.0)
            for c, (a, b) in enumerate(PAIRS):
                first, second = halves_of(x[a] * spring[b])
                prods[r * 64 : r * 64 + CAP, c * 256 : c * 256 + 128] = first
                prods[r * 64 : r * 64 + CAP, c * 256 + 128 : c * 256 + 256] = second
            pltpu.make_async_copy(outbuf.at[:, g, rows], out_hbm.at[:, g, rows], out_sem).start()
        sums = lax.dot_general(pick, prods[...], NT, preferred_element_type=F32)
        spread = jnp.concatenate([sums[c : c + 1] * at_hi for c in range(6)], axis=0)
        first, second = halves_of(spread)
        field[...] += lax.dot_general(
            jnp.concatenate([first, second], axis=0), at_lo, NT, preferred_element_type=F32
        )
        return code_x, code_z

    for g in range(2):
        lax.fori_loop(0, 16, functools.partial(arrive, g=g), codes)

    total = (field[:96] + field[96:]) / (WEISSENBERG * DUMB)
    stress = [
        jnp.concatenate([total[16 * c : 16 * c + 8], total[16 * c + 8 : 16 * c + 16]], axis=1) for c in range(6)
    ]
    for k in range(3):
        sx[k] = stress[ALONG_X[k]]
        sy[k] = stress[ALONG_Y[k]]

    def stress_copy(slot):
        return pltpu.make_async_remote_copy(
            src_ref=sx if slot < 2 else sy, dst_ref=shx.at[slot] if slot < 2 else shy.at[slot - 2],
            send_sem=hs_sem.at[slot], recv_sem=hr_sem.at[slot],
            device_id=halo_targets[slot], device_id_type=MESH,
        )

    for slot in range(4):
        stress_copy(slot).start()
    for slot in range(4):
        stress_copy(slot).wait()
    for k in range(3):
        fx, fy, fz = stress[ALONG_X[k]], stress[ALONG_Y[k]], stress[ALONG_Z[k]]
        e, w, _, _ = stencil(fx, masked(shx[0, k], 0), masked(shx[1, k], 1), fx, fx)
        _, _, n, s = stencil(fy, fy, fy, masked(shy[0, k], 2), masked(shy[1, k], 3))
        u, d = along_z(fz)
        dv[ens, k] = 0.5 * (e - w) + 0.5 * (n - s) + 0.5 * (u - d)

    def dv_copy(k):
        return pltpu.make_async_remote_copy(
            src_ref=dv.at[ens], dst_ref=dv.at[ens], send_sem=ds_sem.at[k], recv_sem=dr_sem.at[k],
            device_id=(lax.rem(ens + k, n_ens), cx, cy), device_id_type=MESH,
        )

    def dv_arrival(k):
        source = lax.rem(ens + n_ens - k, n_ens)
        pltpu.make_async_copy(dv.at[source], dv.at[source], dr_sem.at[k]).wait()

    for k in range(1, n_ens):
        dv_copy(k).start()
    for k in range(1, n_ens):
        dv_arrival(k)
    vout_ref[...] = base[...] + TIME_STEP * (dv[0] + dv[1] + dv[2] + dv[3])

    for k in range(1, n_ens):
        dv_copy(k).wait_send()

    def sent(i, carry):
        for g in range(2):
            for r in range(2):
                pltpu.make_async_copy(sendbuf.at[g, i, r], sendbuf.at[g, i, r], ssem.at[g, i, r]).wait()
                pltpu.make_async_copy(labsend.at[g, i, r], labsend.at[g, i, r], lssem.at[g, i, r]).wait()
        return carry

    lax.fori_loop(0, 15, sent, 0)
    for g in range(2):
        pltpu.make_async_copy(sendbuf.at[g, 15, 1], sendbuf.at[g, 15, 1], ssem.at[g, 15, 1]).wait()
        pltpu.make_async_copy(labsend.at[g, 15, 1], labsend.at[g, 15, 1], lssem.at[g, 15, 1]).wait()
    pltpu.make_async_copy(outbuf, out_hbm, out_sem).wait()


def on_device(conformations, fill_counts, dest_slots, dest_cells, velocity, noise):
    _, groups, blocks, slots = conformations.shape
    places = noise.shape[2]
    vmem = pl.BlockSpec(memory_space=pltpu.VMEM)
    hbm = pl.BlockSpec(memory_space=pl.ANY)
    tile = velocity.shape
    dma = pltpu.SemaphoreType.DMA
    return pl.pallas_call(
        kernel,
        out_shape=(
            jax.ShapeDtypeStruct(noise.shape, F32),
            jax.ShapeDtypeStruct(velocity.shape, F32),
        ),
        in_specs=[hbm, vmem, vmem, vmem, vmem, hbm],
        out_specs=(hbm, vmem),
        scratch_shapes=[
            pltpu.VMEM(conformations.shape, F32),
            pltpu.VMEM((groups, blocks, 3 * slots), BF16),
            pltpu.VMEM((groups, blocks, 3 * slots), BF16),
            pltpu.VMEM((groups, 16, 2, 3, CAP, slots), F32),
            pltpu.VMEM((groups, 16, 2, 3, CAP, slots), F32),
            pltpu.VMEM((groups, 16, 2, 1, 128), F32),
            pltpu.VMEM((groups, 16, 2, 1, 128), F32),
            pltpu.VMEM(noise.shape, F32),
            pltpu.VMEM(noise.shape, F32),
            pltpu.VMEM((4,) + tile, F32),
            pltpu.VMEM((288, 128), BF16),
            pltpu.VMEM((16, 128), F32),
            pltpu.VMEM((128, 12 * 128), BF16),
            pltpu.VMEM((192, 128), F32),
            pltpu.VMEM(tile, F32),
            pltpu.VMEM(tile, F32),
            pltpu.VMEM((2,) + tile, F32),
            pltpu.VMEM((2,) + tile, F32),
            pltpu.VMEM((4,) + tile, F32),
            pltpu.VMEM(tile, F32),
            dma((2,)), dma, dma,
            dma((groups, 16, 2)), dma((groups, 16, 2)),
            dma((groups, 16, 2)), dma((groups, 16, 2)),
            dma((4,)), dma((4,)), dma((4,)), dma((4,)), dma((4,)), dma((4,)),
        ],
        compiler_params=pltpu.CompilerParams(
            collective_id=0, has_side_effects=True, vmem_limit_bytes=52 * 2**20
        ),
    )(conformations, fill_counts, dest_slots, dest_cells, velocity, noise)


def solution(mesh):
    placed = (
        P(None, "ens", ("cx", "cy"), None),
        P("ens", ("cx", "cy")),
        P("ens", ("cx", "cy")),
        P("ens", ("cx", "cy")),
        P(None, "cx", "cy"),
        P(None, "ens", ("cx", "cy"), None),
    )
    return jax.shard_map(
        on_device,
        mesh=mesh,
        in_specs=placed,
        out_specs=(P(None, "ens", ("cx", "cy"), None), P(None, "cx", "cy")),
        check_vma=False,
    )
```

```python
import functools
import math

import jax
import jax.numpy as jnp
from jax import lax
from jax.experimental import pallas as pl
from jax.experimental.pallas import tpu as pltpu
from jax.sharding import PartitionSpec as P

DUMB = 64
NZ = 64
CAP = 48
TIME_STEP = 0.02
WEISSENBERG = 0.5
EXTENSION = 50.0
VISCOSITY = 1.0

PAIRS = ((0, 0), (1, 1), (2, 2), (0, 1), (0, 2), (1, 2))
ALONG_X = (0, 3, 4)
ALONG_Y = (3, 1, 5)
ALONG_Z = (4, 5, 2)

MESH = pl.DeviceIdType.MESH
F32 = jnp.float32
BF16 = jnp.bfloat16

OFFSETS = (
    (2, 2), (2, 1), (1, 2), (2, 3), (3, 2), (2, 0), (0, 2), (1, 1),
    (3, 3), (1, 3), (3, 1), (1, 0), (3, 0), (0, 1), (0, 3),
)
CODE_X = sum(dx * 4**i for i, (dx, _) in enumerate(OFFSETS))
CODE_Z = sum(dz * 4**i for i, (_, dz) in enumerate(OFFSETS))
HALVES = 2
PART = CAP // HALVES
NT = (((1,), (1,)), ((), ()))


def halves_of(values):
    high = values.astype(BF16)
    return high, (values - high.astype(F32)).astype(BF16)


def stencil(field, west, east, south, north):
    row = lax.broadcasted_iota(jnp.int32, field.shape, 0)
    lane = lax.broadcasted_iota(jnp.int32, field.shape, 1)
    rows, width = field.shape
    east_side = jnp.where(row == rows - 1, pltpu.roll(east, rows - 1, 0), pltpu.roll(field, rows - 1, 0))
    west_side = jnp.where(row == 0, pltpu.roll(west, 1, 0), pltpu.roll(field, 1, 0))
    north_side = jnp.where(
        lane >= width - NZ, pltpu.roll(north, width - NZ, 1), pltpu.roll(field, width - NZ, 1)
    )
    south_side = jnp.where(lane < NZ, pltpu.roll(south, NZ, 1), pltpu.roll(field, NZ, 1))
    return east_side, west_side, north_side, south_side


def along_z(field):
    lane = lax.rem(lax.broadcasted_iota(jnp.int32, field.shape, 1), NZ)
    width = field.shape[1]
    upper = jnp.where(lane < NZ - 1, pltpu.roll(field, width - 1, 1), 0.0)
    lower = jnp.where(lane > 0, pltpu.roll(field, 1, 1), 0.0)
    return upper, lower


def kernel(
    conf_hbm, fill_hbm, dest_hbm, cell_hbm, vel_hbm, noise_hbm,
    out_ref, vout_ref,
    conf, fill_ref, dest_ref, cell_ref, vel_ref, noise, high, low, sendbuf, recv, labmat, labsend, labrecv, columns,
    vhalo, table, rowbuf, prods, field, sx, sy, shx, shy, dv, base,
    conf_sem, in_sem, noise_sem, ssem, rsem, lssem, lrsem, vs_sem, vr_sem, hs_sem, hr_sem, ds_sem, dr_sem,
):
    ens = lax.axis_index("ens")
    cx = lax.axis_index("cx")
    cy = lax.axis_index("cy")
    my_x = lax.div(cx, 2)
    core = lax.rem(cx, 2)
    n_ens = 4

    def conf_copy(g):
        return pltpu.make_async_copy(conf_hbm.at[:, g], conf.at[:, g], conf_sem.at[g])

    small = [
        pltpu.make_async_copy(source, target, in_sem.at[k])
        for k, (source, target) in enumerate(
            ((dest_hbm, dest_ref), (vel_hbm, vel_ref), (fill_hbm, fill_ref), (cell_hbm, cell_ref))
        )
    ]
    conf_copy(0).start()
    for copy in small:
        copy.start()
    conf_copy(1).start()
    noise_copy = pltpu.make_async_copy(noise_hbm, noise, noise_sem)
    noise_copy.start()

    east_id = (ens, lax.rem(cx + 1, 8), cy)
    west_id = (ens, lax.rem(cx + 7, 8), cy)
    north_id = (ens, cx, lax.rem(cy + 1, 4))
    south_id = (ens, cx, lax.rem(cy + 3, 4))

    def chip(dx, dz, r):
        return (ens, lax.rem(my_x + dx, 4) * 2 + lax.rem(core + r, 2), lax.rem(cy + dz, 4))

    barrier = pltpu.get_barrier_semaphore()
    for dx, dz in OFFSETS:
        for r in range(2):
            pl.semaphore_signal(barrier, inc=1, device_id=chip(dx, dz, r), device_id_type=MESH)
    pl.semaphore_signal(barrier, inc=1, device_id=chip(0, 0, 1), device_id_type=MESH)
    for k in range(1, n_ens):
        pl.semaphore_signal(
            barrier, inc=1, device_id=(lax.rem(ens + k, n_ens), cx, cy), device_id_type=MESH
        )

    def split(g):
        for a in range(3):
            first, second = halves_of(conf[a, g])
            high[g, :, a * 128 : (a + 1) * 128] = first
            low[g, :, a * 128 : (a + 1) * 128] = second

    blocks = conf.shape[2]
    row48 = lax.broadcasted_iota(jnp.int32, (CAP, blocks), 0)
    row64 = lax.broadcasted_iota(jnp.int32, (64, blocks), 0)
    row64 = jnp.where(row64 < CAP, row64, 2**20)
    lane128 = lax.broadcasted_iota(jnp.int32, (1, 128), 1)

    field[...] = jnp.zeros_like(field)
    rowbuf[...] = jnp.zeros_like(rowbuf)
    conf_copy(0).wait()
    split(0)
    for copy in small:
        copy.wait()
    pl.semaphore_wait(barrier, 31 + n_ens - 1)

    def data_copy(g, i, r, h, target):
        rows = pl.ds(h * PART, PART)
        return pltpu.make_async_remote_copy(
            src_ref=sendbuf.at[g, i, r, :, rows], dst_ref=recv.at[g, i, r, :, rows],
            send_sem=ssem.at[g, i, r], recv_sem=rsem.at[g, i, r],
            device_id=target, device_id_type=MESH,
        )

    def label_copy(g, i, r, target):
        return pltpu.make_async_remote_copy(
            src_ref=labsend.at[g, i, r], dst_ref=labrecv.at[g, i, r],
            send_sem=lssem.at[g, i, r], recv_sem=lrsem.at[g, i, r],
            device_id=target, device_id_type=MESH,
        )

    def batch_targets(carry):
        code_x, code_z = carry
        targets = []
        for _ in range(4):
            dx, dz = lax.rem(code_x, 4), lax.rem(code_z, 4)
            code_x, code_z = lax.div(code_x, 4), lax.div(code_z, 4)
            targets += [chip(dx, dz, 0), chip(dx, dz, 1)]
        return targets, (code_x, code_z)

    def one_hot(dest, targets, rows):
        return jnp.concatenate(
            [
                jnp.where(dest - (target[1] * 4 + target[2]) * CAP == rows, 1.0, 0.0).astype(BF16)
                for target in targets
            ],
            axis=0,
        )

    def pack_batch(q, carry, g):
        targets, carry = batch_targets(carry)
        onehot = one_hot(dest_ref[g : g + 1, :], targets, row48)
        packed = jnp.dot(onehot, high[g], preferred_element_type=F32) + jnp.dot(
            onehot, low[g], preferred_element_type=F32
        )
        for n in range(8):
            for a in range(3):
                sendbuf[g, 4 * q + n // 2, n % 2, a] = packed[
                    n * CAP : (n + 1) * CAP, a * 128 : (a + 1) * 128
                ]
        for h in range(HALVES):
            for n in range(6):
                data_copy(g, 4 * q + n // 2, n % 2, h, targets[n]).start()

        @pl.when(q < 3)
        def _():
            for h in range(HALVES):
                for n in range(6, 8):
                    data_copy(g, 4 * q + n // 2, n % 2, h, targets[n]).start()

        @pl.when(q == 3)
        def _():
            for h in range(HALVES):
                data_copy(g, 15, 1, h, targets[7]).start()
            pltpu.make_async_copy(sendbuf.at[g, 15, 0], recv.at[g, 15, 0], rsem.at[g, 15, 0]).start()

        return carry

    codes = (jnp.int32(CODE_X), jnp.int32(CODE_Z))
    later_codes = (jnp.int32(CODE_X // 4**8), jnp.int32(CODE_Z // 4**8))
    lax.fori_loop(0, 2, functools.partial(pack_batch, g=0), codes)

    def vel_copy(slot, target):
        return pltpu.make_async_remote_copy(
            src_ref=vel_ref, dst_ref=vhalo.at[slot], send_sem=vs_sem.at[slot], recv_sem=vr_sem.at[slot],
            device_id=target, device_id_type=MESH,
        )

    halo_targets = (east_id, west_id, north_id, south_id)
    for slot in range(4):
        vel_copy(slot, halo_targets[slot]).start()

    lab_row = lax.broadcasted_iota(jnp.int32, (16, 128), 0)
    block_lane = lax.broadcasted_iota(jnp.int32, (128, 128), 1).astype(F32)
    pick_row = lax.broadcasted_iota(jnp.int32, (16, 12 * 128), 0)
    pick_pair = lax.div(lax.broadcasted_iota(jnp.int32, (16, 12 * 128), 1), 256)
    pick = jnp.where((pick_row == pick_pair + 3) | (pick_row == pick_pair + 9), 1.0, 0.0).astype(BF16)

    def label_rows(k, carry, g):
        rows = pl.ds(pl.multiple_of(k * 128, 128), 128)
        fill = fill_ref[g : g + 1, rows].astype(F32)
        cell = cell_ref[g : g + 1, rows]
        rowbuf[0:1] = fill
        live = block_lane < rowbuf[...].T[:, 0:1]
        x = [jnp.where(live, conf[a, g, rows], 0.0) for a in range(3)]
        inverse = 1.0 / (1.0 - (x[0] * x[0] + x[1] * x[1] + x[2] * x[2]) / EXTENSION)
        spring = [x[a] * inverse for a in range(3)]
        for c, (a, b) in enumerate(PAIRS):
            first, second = halves_of(x[a] * spring[b])
            prods[:, c * 256 : c * 256 + 128] = first
            prods[:, c * 256 + 128 : c * 256 + 256] = second
        sums = lax.dot_general(pick, prods[...], NT, preferred_element_type=F32)
        first = sums.astype(BF16).astype(F32)
        cell_hi = lax.div(cell, 128).astype(F32)
        cell_lo = lax.rem(cell, 128).astype(F32)
        rest = jnp.where(lab_row < 9, first, jnp.where(lab_row < 15, sums - first, 0.0))
        labmat[g, :, rows] = jnp.where(
            lab_row == 0, fill, jnp.where(lab_row == 1, cell_hi, jnp.where(lab_row == 2, cell_lo, rest))
        ).astype(BF16)
        return carry

    conf_copy(1).wait()
    for g in range(2):
        lax.fori_loop(0, blocks // 128, functools.partial(label_rows, g=g), 0)

    def label_batch(q, carry, g):
        targets, carry = batch_targets(carry)
        onehot = one_hot(dest_ref[g : g + 1, :], targets, row64)
        told = lax.dot_general(labmat[g], onehot, NT, preferred_element_type=F32)
        top = jnp.concatenate([told[0:1], told[1:2] * 128.0 + told[2:3], told[3:5] + told[9:11]], axis=0)
        bottom = told[5:9] + told[11:15]
        for m in range(4):
            upper, lower = top[:, m * 128 : (m + 1) * 128], bottom[:, m * 128 : (m + 1) * 128]
            labsend[g, 4 * q + m, 0] = jnp.where(lane128 < 64, upper, pltpu.roll(lower, 64, 1))
            labsend[g, 4 * q + m, 1] = jnp.where(lane128 < 64, pltpu.roll(upper, 64, 1), lower)
        for n in range(6):
            label_copy(g, 4 * q + n // 2, n % 2, targets[n]).start()

        @pl.when(q < 3)
        def _():
            for n in range(6, 8):
                label_copy(g, 4 * q + n // 2, n % 2, targets[n]).start()

        @pl.when(q == 3)
        def _():
            label_copy(g, 15, 1, targets[7]).start()
            pltpu.make_async_copy(labsend.at[g, 15, 0], labrecv.at[g, 15, 0], lrsem.at[g, 15, 0]).start()

        return carry

    for g in range(2):
        lax.fori_loop(0, 4, functools.partial(label_batch, g=g), codes)

    lax.fori_loop(2, 4, functools.partial(pack_batch, g=0), later_codes)
    split(1)
    lax.fori_loop(0, 4, functools.partial(pack_batch, g=1), codes)

    for slot in range(4):
        vel_copy(slot, halo_targets[slot]).wait()
    inside = (cx > 0, cx < 7, cy > 0, cy < 3)

    def masked(tile, k):
        return jnp.where(inside[k], tile, 0.0)

    for a in range(3):
        f = vel_ref[a]
        e, w, n, s = stencil(f, *(masked(vhalo[k, a], k) for k in range(4)))
        u, d = along_z(f)
        base[a] = f + TIME_STEP * VISCOSITY * (e + w + n + s + u + d - 6.0 * f)
        for b, slope in enumerate((0.5 * (e - w), 0.5 * (n - s), 0.5 * (u - d))):
            first, second = halves_of(jnp.concatenate([slope[:, :128], slope[:, 128:]], axis=0))
            top = (3 * a + b) * 16
            table[top : top + 16] = first
            table[144 + top : 144 + top + 16] = second

    square = lax.broadcasted_iota(jnp.int32, (128, 128), 0)
    row_hi = lax.broadcasted_iota(jnp.int32, (16, 128), 0)

    def read_labels(i, carry, g):
        for r in range(2):
            pltpu.make_async_copy(labrecv.at[g, i, r], labrecv.at[g, i, r], lrsem.at[g, i, r]).wait()
        lab0, lab1 = labrecv[g, i, 0], labrecv[g, i, 1]
        upper = jnp.where(lane128 < 64, lab0, pltpu.roll(lab1, 64, 1))
        lower = jnp.where(lane128 < 64, pltpu.roll(lab0, 64, 1), lab1)
        cells = upper[1:2].astype(jnp.int32)
        cell_lo = lax.rem(cells, 128)
        cell_hi = lax.div(cells, 128)
        cell_hi = lax.rem(cell_hi, 2) * 8 + lax.div(cell_hi, 2)
        at_lo = jnp.where(square == cell_lo, 1.0, 0.0).astype(BF16)
        at_hi = jnp.where(row_hi == cell_hi, 1.0, 0.0)
        looked = jnp.dot(table[...], at_lo, preferred_element_type=F32)
        looked = looked[:144] + looked[144:]
        for c in range(9):
            rowbuf[c : c + 1] = jnp.sum(looked[16 * c : 16 * c + 16] * at_hi, axis=0, keepdims=True)
        rowbuf[9:10] = upper[0:1]
        columns[g, i] = rowbuf[...].T
        sums = [upper[2:3], upper[3:4]] + [lower[c : c + 1] for c in range(4)]
        spread = jnp.concatenate([sums[c] * at_hi for c in range(6)], axis=0)
        first, second = halves_of(spread)
        field[...] += lax.dot_general(
            jnp.concatenate([first, second], axis=0), at_lo, NT, preferred_element_type=F32
        )
        return carry

    for g in range(2):
        lax.fori_loop(0, 16, functools.partial(read_labels, g=g), 0)

    total = (field[:96] + field[96:]) / (WEISSENBERG * DUMB)
    stress = [
        jnp.concatenate([total[16 * c : 16 * c + 8], total[16 * c + 8 : 16 * c + 16]], axis=1) for c in range(6)
    ]
    for k in range(3):
        sx[k] = stress[ALONG_X[k]]
        sy[k] = stress[ALONG_Y[k]]
        u, d = along_z(stress[ALONG_Z[k]])
        dv[ens, k] = 0.5 * (u - d)

    def stress_copy(slot):
        return pltpu.make_async_remote_copy(
            src_ref=sx if slot < 2 else sy, dst_ref=shx.at[slot] if slot < 2 else shy.at[slot - 2],
            send_sem=hs_sem.at[slot], recv_sem=hr_sem.at[slot],
            device_id=halo_targets[slot], device_id_type=MESH,
        )

    for slot in range(4):
        stress_copy(slot).start()

    noise_copy.wait()
    slot_lane = lax.broadcasted_iota(jnp.int32, (CAP, 128), 1).astype(F32)

    def arrive(j, carry, g):
        code_x, code_z = carry
        own = j == 0
        i = lax.rem(j + 15, 16)
        dx = jnp.where(own, 0, lax.rem(code_x, 4))
        dz = jnp.where(own, 0, lax.rem(code_z, 4))
        code_x = jnp.where(own, code_x, lax.div(code_x, 4))
        code_z = jnp.where(own, code_z, lax.div(code_z, 4))
        for r in range(2):
            pltpu.make_async_copy(recv.at[g, i, r], recv.at[g, i, r], rsem.at[g, i, r]).wait()
        for r in range(2):
            source = (lax.rem(my_x + 4 - dx, 4) * 2 + lax.rem(core + r, 2)) * 4 + lax.rem(cy + 4 - dz, 4)
            rows = pl.ds(pl.multiple_of(source * CAP, CAP), CAP)
            here = columns[g, i, r * 64 : r * 64 + CAP]
            live = slot_lane < here[:, 9:10]
            x = [jnp.where(live, recv[g, i, r, a], 0.0) for a in range(3)]
            inverse = 1.0 / (1.0 - (x[0] * x[0] + x[1] * x[1] + x[2] * x[2]) / EXTENSION)
            for a in range(3):
                stretch = sum(here[:, 3 * a + b : 3 * a + b + 1] * x[b] for b in range(3))
                stepped = (
                    x[a]
                    + TIME_STEP * (stretch - x[a] * inverse / (2.0 * WEISSENBERG))
                    + math.sqrt(TIME_STEP / WEISSENBERG) * noise[a, g, rows]
                )
                out_ref[a, g, rows] = jnp.where(live, stepped, 0.0)
        return code_x, code_z

    lax.fori_loop(0, 16, functools.partial(arrive, g=0), codes)

    for slot in range(4):
        stress_copy(slot).wait()
    for k in range(3):
        fx, fy = sx[k], sy[k]
        e, w, _, _ = stencil(fx, masked(shx[0, k], 0), masked(shx[1, k], 1), fx, fx)
        _, _, n, s = stencil(fy, fy, fy, masked(shy[0, k], 2), masked(shy[1, k], 3))
        dv[ens, k] = dv[ens, k] + 0.5 * (e - w) + 0.5 * (n - s)

    def dv_copy(k):
        return pltpu.make_async_remote_copy(
            src_ref=dv.at[ens], dst_ref=dv.at[ens], send_sem=ds_sem.at[k], recv_sem=dr_sem.at[k],
            device_id=(lax.rem(ens + k, n_ens), cx, cy), device_id_type=MESH,
        )

    def dv_arrival(k):
        source = lax.rem(ens + n_ens - k, n_ens)
        pltpu.make_async_copy(dv.at[source], dv.at[source], dr_sem.at[k]).wait()

    for k in range(1, n_ens):
        dv_copy(k).start()

    lax.fori_loop(0, 16, functools.partial(arrive, g=1), codes)

    for k in range(1, n_ens):
        dv_arrival(k)
    vout_ref[...] = base[...] + TIME_STEP * (dv[0] + dv[1] + dv[2] + dv[3])

    for k in range(1, n_ens):
        dv_copy(k).wait_send()

    def sent(i, carry):
        for g in range(2):
            for r in range(2):
                pltpu.make_async_copy(sendbuf.at[g, i, r], sendbuf.at[g, i, r], ssem.at[g, i, r]).wait()
                pltpu.make_async_copy(labsend.at[g, i, r], labsend.at[g, i, r], lssem.at[g, i, r]).wait()
        return carry

    lax.fori_loop(0, 15, sent, 0)
    for g in range(2):
        pltpu.make_async_copy(sendbuf.at[g, 15, 1], sendbuf.at[g, 15, 1], ssem.at[g, 15, 1]).wait()
        pltpu.make_async_copy(labsend.at[g, 15, 1], labsend.at[g, 15, 1], lssem.at[g, 15, 1]).wait()


def on_device(conformations, fill_counts, dest_slots, dest_cells, velocity, noise):
    _, groups, blocks, slots = conformations.shape
    vmem = pl.BlockSpec(memory_space=pltpu.VMEM)
    hbm = pl.BlockSpec(memory_space=pl.ANY)
    tile = velocity.shape
    arguments = (conformations, fill_counts, dest_slots, dest_cells, velocity, noise)
    dma = pltpu.SemaphoreType.DMA
    return pl.pallas_call(
        kernel,
        out_shape=(
            pltpu.VMEM(noise.shape, F32),
            pltpu.VMEM(velocity.shape, F32),
        ),
        in_specs=[hbm] * 6,
        out_specs=(vmem, vmem),
        scratch_shapes=[
            pltpu.VMEM(conformations.shape, F32),
            pltpu.VMEM(fill_counts.shape, jnp.int32),
            pltpu.VMEM(fill_counts.shape, jnp.int32),
            pltpu.VMEM(fill_counts.shape, jnp.int32),
            pltpu.VMEM(tile, F32),
            pltpu.VMEM(noise.shape, F32),
            pltpu.VMEM((groups, blocks, 3 * slots), BF16),
            pltpu.VMEM((groups, blocks, 3 * slots), BF16),
            pltpu.VMEM((groups, 16, 2, 3, CAP, slots), F32),
            pltpu.VMEM((groups, 16, 2, 3, CAP, slots), F32),
            pltpu.VMEM((groups, 16, blocks), BF16),
            pltpu.VMEM((groups, 16, 2, 4, 128), F32),
            pltpu.VMEM((groups, 16, 2, 4, 128), F32),
            pltpu.VMEM((groups, 16, 128, 16), F32),
            pltpu.VMEM((4,) + tile, F32),
            pltpu.VMEM((288, 128), BF16),
            pltpu.VMEM((16, 128), F32),
            pltpu.VMEM((128, 12 * 128), BF16),
            pltpu.VMEM((192, 128), F32),
            pltpu.VMEM(tile, F32),
            pltpu.VMEM(tile, F32),
            pltpu.VMEM((2,) + tile, F32),
            pltpu.VMEM((2,) + tile, F32),
            pltpu.VMEM((4,) + tile, F32),
            pltpu.VMEM(tile, F32),
            dma((2,)), dma((4,)), dma,
            dma((groups, 16, 2)), dma((groups, 16, 2)),
            dma((groups, 16, 2)), dma((groups, 16, 2)),
            dma((4,)), dma((4,)), dma((4,)), dma((4,)), dma((4,)), dma((4,)),
        ],
        compiler_params=pltpu.CompilerParams(
            collective_id=0, has_side_effects=True, vmem_limit_bytes=40 * 2**20
        ),
    )(*(pltpu.with_memory_space_constraint(x, pltpu.HBM) for x in arguments))


def solution(mesh):
    placed = (
        P(None, "ens", ("cx", "cy"), None),
        P("ens", ("cx", "cy")),
        P("ens", ("cx", "cy")),
        P("ens", ("cx", "cy")),
        P(None, "cx", "cy"),
        P(None, "ens", ("cx", "cy"), None),
    )
    return jax.shard_map(
        on_device,
        mesh=mesh,
        in_specs=placed,
        out_specs=(P(None, "ens", ("cx", "cy"), None), P(None, "cx", "cy")),
        check_vma=False,
    )
```

```python
import functools
import math

import jax
import jax.numpy as jnp
from jax import lax
from jax.experimental import pallas as pl
from jax.experimental.pallas import tpu as pltpu
from jax.sharding import PartitionSpec as P

DUMB = 64
NZ = 64
CAP = 48
TIME_STEP = 0.02
WEISSENBERG = 0.5
EXTENSION = 50.0
VISCOSITY = 1.0

PAIRS = ((0, 0), (1, 1), (2, 2), (0, 1), (0, 2), (1, 2))
ALONG_X = (0, 3, 4)
ALONG_Y = (3, 1, 5)
ALONG_Z = (4, 5, 2)

MESH = pl.DeviceIdType.MESH
F32 = jnp.float32
BF16 = jnp.bfloat16

OFFSETS = (
    (2, 2), (2, 1), (1, 2), (2, 3), (3, 2), (2, 0), (0, 2), (1, 1),
    (3, 3), (1, 3), (3, 1), (1, 0), (3, 0), (0, 1), (0, 3),
)
CODE_X = sum(dx * 4**i for i, (dx, _) in enumerate(OFFSETS))
CODE_Z = sum(dz * 4**i for i, (_, dz) in enumerate(OFFSETS))
HALVES = 2
PART = CAP // HALVES
NT = (((1,), (1,)), ((), ()))


def halves_of(values):
    high = values.astype(BF16)
    return high, (values - high.astype(F32)).astype(BF16)


def stencil(field, west, east, south, north):
    row = lax.broadcasted_iota(jnp.int32, field.shape, 0)
    lane = lax.broadcasted_iota(jnp.int32, field.shape, 1)
    rows, width = field.shape
    east_side = jnp.where(row == rows - 1, pltpu.roll(east, rows - 1, 0), pltpu.roll(field, rows - 1, 0))
    west_side = jnp.where(row == 0, pltpu.roll(west, 1, 0), pltpu.roll(field, 1, 0))
    north_side = jnp.where(
        lane >= width - NZ, pltpu.roll(north, width - NZ, 1), pltpu.roll(field, width - NZ, 1)
    )
    south_side = jnp.where(lane < NZ, pltpu.roll(south, NZ, 1), pltpu.roll(field, NZ, 1))
    return east_side, west_side, north_side, south_side


def along_z(field):
    lane = lax.rem(lax.broadcasted_iota(jnp.int32, field.shape, 1), NZ)
    width = field.shape[1]
    upper = jnp.where(lane < NZ - 1, pltpu.roll(field, width - 1, 1), 0.0)
    lower = jnp.where(lane > 0, pltpu.roll(field, 1, 1), 0.0)
    return upper, lower


def kernel(
    conf_hbm, fill_hbm, dest_hbm, cell_hbm, vel_hbm, noise_hbm,
    out_ref, vout_ref,
    conf, fill_ref, dest_ref, cell_ref, vel_ref, noise, high, low, sendbuf, recv, labels, labsend, labrecv, columns,
    vhalo, table, rowbuf, field, sx, sy, shx, shy, dv, base,
    conf_sem, in_sem, noise_sem, ssem, rsem, lssem, lrsem, vs_sem, vr_sem, hs_sem, hr_sem, ds_sem, dr_sem,
):
    ens = lax.axis_index("ens")
    cx = lax.axis_index("cx")
    cy = lax.axis_index("cy")
    my_x = lax.div(cx, 2)
    core = lax.rem(cx, 2)
    n_ens = 4

    def conf_copy(g):
        return pltpu.make_async_copy(conf_hbm.at[:, g], conf.at[:, g], conf_sem.at[g])

    small = [
        pltpu.make_async_copy(source, target, in_sem.at[k])
        for k, (source, target) in enumerate(
            ((dest_hbm, dest_ref), (vel_hbm, vel_ref), (fill_hbm, fill_ref), (cell_hbm, cell_ref))
        )
    ]
    conf_copy(0).start()
    for copy in small:
        copy.start()
    conf_copy(1).start()
    noise_copy = pltpu.make_async_copy(noise_hbm, noise, noise_sem)
    noise_copy.start()

    east_id = (ens, lax.rem(cx + 1, 8), cy)
    west_id = (ens, lax.rem(cx + 7, 8), cy)
    north_id = (ens, cx, lax.rem(cy + 1, 4))
    south_id = (ens, cx, lax.rem(cy + 3, 4))

    def chip(dx, dz, r):
        return (ens, lax.rem(my_x + dx, 4) * 2 + lax.rem(core + r, 2), lax.rem(cy + dz, 4))

    barrier = pltpu.get_barrier_semaphore()
    for dx, dz in OFFSETS:
        for r in range(2):
            pl.semaphore_signal(barrier, inc=1, device_id=chip(dx, dz, r), device_id_type=MESH)
    pl.semaphore_signal(barrier, inc=1, device_id=chip(0, 0, 1), device_id_type=MESH)
    for k in range(1, n_ens):
        pl.semaphore_signal(
            barrier, inc=1, device_id=(lax.rem(ens + k, n_ens), cx, cy), device_id_type=MESH
        )

    def split(g):
        for a in range(3):
            first, second = halves_of(conf[a, g])
            high[g, :, a * 128 : (a + 1) * 128] = first
            low[g, :, a * 128 : (a + 1) * 128] = second

    blocks = conf.shape[2]
    row48 = lax.broadcasted_iota(jnp.int32, (CAP, blocks), 0)
    lane128 = lax.broadcasted_iota(jnp.int32, (1, 128), 1)

    field[...] = jnp.zeros_like(field)
    rowbuf[...] = jnp.zeros_like(rowbuf)
    conf_copy(0).wait()
    split(0)
    for copy in small:
        copy.wait()
    pl.semaphore_wait(barrier, 31 + n_ens - 1)

    def vel_copy(slot, target):
        return pltpu.make_async_remote_copy(
            src_ref=vel_ref, dst_ref=vhalo.at[slot], send_sem=vs_sem.at[slot], recv_sem=vr_sem.at[slot],
            device_id=target, device_id_type=MESH,
        )

    halo_targets = (east_id, west_id, north_id, south_id)
    for slot in range(4):
        vel_copy(slot, halo_targets[slot]).start()

    def data_copy(g, i, r, h, target):
        rows = pl.ds(h * PART, PART)
        return pltpu.make_async_remote_copy(
            src_ref=sendbuf.at[g, i, r, :, rows], dst_ref=recv.at[g, i, r, :, rows],
            send_sem=ssem.at[g, i, r], recv_sem=rsem.at[g, i, r],
            device_id=target, device_id_type=MESH,
        )

    def label_copy(g, i, r, target):
        return pltpu.make_async_remote_copy(
            src_ref=labsend.at[g, i, r], dst_ref=labrecv.at[g, i, r],
            send_sem=lssem.at[g, i, r], recv_sem=lrsem.at[g, i, r],
            device_id=target, device_id_type=MESH,
        )

    def batch_targets(carry):
        code_x, code_z = carry
        targets = []
        for _ in range(4):
            dx, dz = lax.rem(code_x, 4), lax.rem(code_z, 4)
            code_x, code_z = lax.div(code_x, 4), lax.div(code_z, 4)
            targets += [chip(dx, dz, 0), chip(dx, dz, 1)]
        return targets, (code_x, code_z)

    def one_hot(dest, targets, rows):
        return jnp.concatenate(
            [
                jnp.where(dest - (target[1] * 4 + target[2]) * CAP == rows, 1.0, 0.0).astype(BF16)
                for target in targets
            ],
            axis=0,
        )

    def pack_batch(q, carry, g):
        targets, carry = batch_targets(carry)
        onehot = one_hot(dest_ref[g : g + 1, :], targets, row48)
        packed = jnp.dot(onehot, high[g], preferred_element_type=F32) + jnp.dot(
            onehot, low[g], preferred_element_type=F32
        )
        for n in range(8):
            for a in range(3):
                sendbuf[g, 4 * q + n // 2, n % 2, a] = packed[
                    n * CAP : (n + 1) * CAP, a * 128 : (a + 1) * 128
                ]
        for h in range(HALVES):
            for n in range(6):
                data_copy(g, 4 * q + n // 2, n % 2, h, targets[n]).start()

        @pl.when(q < 3)
        def _():
            for h in range(HALVES):
                for n in range(6, 8):
                    data_copy(g, 4 * q + n // 2, n % 2, h, targets[n]).start()

        @pl.when(q == 3)
        def _():
            for h in range(HALVES):
                data_copy(g, 15, 1, h, targets[7]).start()
            pltpu.make_async_copy(sendbuf.at[g, 15, 0], recv.at[g, 15, 0], rsem.at[g, 15, 0]).start()

        return carry

    codes = (jnp.int32(CODE_X), jnp.int32(CODE_Z))

    def send_blocks(g, first, last):
        start = tuple(jnp.int32(code // 4 ** (4 * first)) for code in (CODE_X, CODE_Z))
        lax.fori_loop(first, last, functools.partial(pack_batch, g=g), start)

    send_blocks(0, 0, 1)

    lab_row = lax.broadcasted_iota(jnp.int32, (8, 128), 0)
    block_lane = lax.broadcasted_iota(jnp.int32, (128, 128), 1)

    def label_rows(k, carry, g):
        rows = pl.ds(pl.multiple_of(k * 128, 128), 128)
        fill = fill_ref[g : g + 1, rows]
        cell = cell_ref[g : g + 1, rows].astype(F32)
        live = block_lane < jnp.broadcast_to(fill, (8, 128)).T[:, 0:1]
        fill = fill.astype(F32)
        x = [jnp.where(live, conf[a, g, rows], 0.0) for a in range(3)]
        inverse = 1.0 / (1.0 - (x[0] * x[0] + x[1] * x[1] + x[2] * x[2]) / EXTENSION)
        spring = [x[a] * inverse for a in range(3)]
        sums = jnp.zeros((128, 128), F32)
        for c, (a, b) in enumerate(PAIRS):
            sums = jnp.where(block_lane == c + 2, jnp.sum(x[a] * spring[b], axis=1, keepdims=True), sums)
        sums = sums.T[:8]
        labels[g, :, rows] = jnp.where(lab_row == 0, fill, jnp.where(lab_row == 1, cell, sums))
        return carry

    conf_copy(1).wait()
    for g in range(2):
        lax.fori_loop(0, blocks // 128, functools.partial(label_rows, g=g), 0)

    row8 = lax.broadcasted_iota(jnp.int32, (8, blocks), 0)
    row128 = lax.broadcasted_iota(jnp.int32, (128, blocks), 0)

    def send_labels(g):
        dest = dest_ref[g : g + 1, :]
        owner = ((dest.astype(F32) + 0.5) * (1.0 / CAP)).astype(jnp.int32)
        slot = dest - owner * CAP
        values = labels[g]
        first = values.astype(BF16).astype(F32)
        terms = (first, values - first)
        told = jnp.zeros((128, 128), F32)
        chips = []
        for p in range(16):
            (_, x0, z0), (_, x1, _) = chip(p // 4, p % 4, 0), chip(p // 4, p % 4, 1)
            chips.append(owner == jnp.where(row8 < 4, x0 * 4 + z0, x1 * 4 + z0))
        for half in range(2):
            where_to = jnp.where(row128 - 64 * half == slot, 1.0, 0.0).astype(BF16)
            for term in terms:
                four = term[4 * half : 4 * half + 4]
                four = jnp.concatenate([four, four], axis=0)
                spread = jnp.concatenate(
                    [
                        jnp.concatenate(
                            [jnp.where(chips[p], four, 0.0), jnp.where(chips[p + 1], four, 0.0)], axis=0
                        ).astype(BF16)
                        for p in range(0, 16, 2)
                    ],
                    axis=0,
                )
                told = told + lax.dot_general(spread, where_to, NT, preferred_element_type=F32)
        for p in range(16):
            for r in range(2):
                labsend[g, p, r] = told[8 * p + 4 * r : 8 * p + 4 * r + 4]
        label_copy(g, 0, 1, chip(0, 0, 1)).start()
        pltpu.make_async_copy(labsend.at[g, 0, 0], labrecv.at[g, 0, 0], lrsem.at[g, 0, 0]).start()

        def start(p, carry):
            for r in range(2):
                label_copy(g, p, r, chip(lax.div(p, 4), lax.rem(p, 4), r)).start()
            return carry

        lax.fori_loop(1, 16, start, 0)

    for g in range(2):
        send_labels(g)

    send_blocks(0, 1, 4)
    split(1)
    send_blocks(1, 0, 1)

    for slot in range(4):
        vel_copy(slot, halo_targets[slot]).wait()
    inside = (cx > 0, cx < 7, cy > 0, cy < 3)

    def masked(tile, k):
        return jnp.where(inside[k], tile, 0.0)

    for a in range(3):
        f = vel_ref[a]
        e, w, n, s = stencil(f, *(masked(vhalo[k, a], k) for k in range(4)))
        u, d = along_z(f)
        base[a] = f + TIME_STEP * VISCOSITY * (e + w + n + s + u + d - 6.0 * f)
        for b, slope in enumerate((0.5 * (e - w), 0.5 * (n - s), 0.5 * (u - d))):
            first, second = halves_of(jnp.concatenate([slope[:, :128], slope[:, 128:]], axis=0))
            top = (3 * a + b) * 16
            table[top : top + 16] = first
            table[144 + top : 144 + top + 16] = second

    square = lax.broadcasted_iota(jnp.int32, (128, 128), 0)
    row_hi = lax.broadcasted_iota(jnp.int32, (16, 128), 0)

    def read_labels(q, carry, g):
        uppers, sums, lows, highs = [], [], [], []
        for m in range(4):
            for r in range(2):
                landed = labrecv.at[g, 4 * q + m, r]
                pltpu.make_async_copy(landed, landed, lrsem.at[g, 4 * q + m, r]).wait()
            lab0, lab1 = labrecv[g, 4 * q + m, 0], labrecv[g, 4 * q + m, 1]
            upper = jnp.where(lane128 < 64, lab0, pltpu.roll(lab1, 64, 1))
            lower = jnp.where(lane128 < 64, pltpu.roll(lab0, 64, 1), lab1)
            cells = upper[1:2].astype(jnp.int32)
            cell_hi = lax.div(cells, 128)
            cell_hi = lax.rem(cell_hi, 2) * 8 + lax.div(cell_hi, 2)
            uppers.append(upper)
            sums.append([upper[2:3], upper[3:4]] + [lower[c : c + 1] for c in range(4)])
            lows.append(jnp.where(square == lax.rem(cells, 128), 1.0, 0.0).astype(BF16))
            highs.append(jnp.where(row_hi == cell_hi, 1.0, 0.0))
        at_lo = jnp.concatenate(lows, axis=1)
        spread = jnp.concatenate(
            [jnp.concatenate([sums[m][c] * highs[m] for c in range(6)], axis=0) for m in range(4)], axis=1
        )
        first, second = halves_of(spread)
        field[...] += lax.dot_general(
            jnp.concatenate([first, second], axis=0), at_lo, NT, preferred_element_type=F32
        )
        looked = jnp.dot(table[...], at_lo, preferred_element_type=F32)
        looked = looked[:144] + looked[144:]
        for m in range(4):
            for c in range(9):
                rowbuf[m, c : c + 1] = jnp.sum(
                    looked[16 * c : 16 * c + 16, 128 * m : 128 * m + 128] * highs[m], axis=0, keepdims=True
                )
            rowbuf[m, 9:10] = uppers[m][0:1]
        for m in range(4):
            columns[g, 4 * q + m] = rowbuf[m].T
        return carry

    for g in range(2):
        lax.fori_loop(0, 4, functools.partial(read_labels, g=g), 0)

    total = (field[:96] + field[96:]) / (WEISSENBERG * DUMB)
    stress = [
        jnp.concatenate([total[16 * c : 16 * c + 8], total[16 * c + 8 : 16 * c + 16]], axis=1) for c in range(6)
    ]
    for k in range(3):
        sx[k] = stress[ALONG_X[k]]
        sy[k] = stress[ALONG_Y[k]]
        u, d = along_z(stress[ALONG_Z[k]])
        dv[ens, k] = 0.5 * (u - d)

    def stress_copy(slot):
        return pltpu.make_async_remote_copy(
            src_ref=sx if slot < 2 else sy, dst_ref=shx.at[slot] if slot < 2 else shy.at[slot - 2],
            send_sem=hs_sem.at[slot], recv_sem=hr_sem.at[slot],
            device_id=halo_targets[slot], device_id_type=MESH,
        )

    for slot in range(4):
        stress_copy(slot).start()

    for slot in range(4):
        stress_copy(slot).wait()
    for k in range(3):
        fx, fy = sx[k], sy[k]
        e, w, _, _ = stencil(fx, masked(shx[0, k], 0), masked(shx[1, k], 1), fx, fx)
        _, _, n, s = stencil(fy, fy, fy, masked(shy[0, k], 2), masked(shy[1, k], 3))
        dv[ens, k] = dv[ens, k] + 0.5 * (e - w) + 0.5 * (n - s)

    def dv_copy(k):
        return pltpu.make_async_remote_copy(
            src_ref=dv.at[ens], dst_ref=dv.at[ens], send_sem=ds_sem.at[k], recv_sem=dr_sem.at[k],
            device_id=(lax.rem(ens + k, n_ens), cx, cy), device_id_type=MESH,
        )

    def dv_arrival(k):
        source = lax.rem(ens + n_ens - k, n_ens)
        pltpu.make_async_copy(dv.at[source], dv.at[source], dr_sem.at[k]).wait()

    for k in range(1, n_ens):
        dv_copy(k).start()


    send_blocks(1, 1, 4)
    noise_copy.wait()
    slot_lane = lax.broadcasted_iota(jnp.int32, (CAP, 128), 1).astype(F32)

    def arrive(j, carry, g):
        code_x, code_z = carry
        own = j == 0
        i = lax.rem(j + 15, 16)
        dx = jnp.where(own, 0, lax.rem(code_x, 4))
        dz = jnp.where(own, 0, lax.rem(code_z, 4))
        code_x = jnp.where(own, code_x, lax.div(code_x, 4))
        code_z = jnp.where(own, code_z, lax.div(code_z, 4))
        for r in range(2):
            pltpu.make_async_copy(recv.at[g, i, r], recv.at[g, i, r], rsem.at[g, i, r]).wait()
        for r in range(2):
            source = (lax.rem(my_x + 4 - dx, 4) * 2 + lax.rem(core + r, 2)) * 4 + lax.rem(cy + 4 - dz, 4)
            rows = pl.ds(pl.multiple_of(source * CAP, CAP), CAP)
            here = columns[g, dx * 4 + dz, r * 64 : r * 64 + CAP]
            live = slot_lane < here[:, 9:10]
            x = [jnp.where(live, recv[g, i, r, a], 0.0) for a in range(3)]
            inverse = 1.0 / (1.0 - (x[0] * x[0] + x[1] * x[1] + x[2] * x[2]) / EXTENSION)
            for a in range(3):
                stretch = sum(here[:, 3 * a + b : 3 * a + b + 1] * x[b] for b in range(3))
                stepped = (
                    x[a]
                    + TIME_STEP * (stretch - x[a] * inverse / (2.0 * WEISSENBERG))
                    + math.sqrt(TIME_STEP / WEISSENBERG) * noise[a, g, rows]
                )
                out_ref[a, g, rows] = jnp.where(live, stepped, 0.0)
        return code_x, code_z

    lax.fori_loop(0, 16, functools.partial(arrive, g=0), codes)

    lax.fori_loop(0, 16, functools.partial(arrive, g=1), codes)

    for k in range(1, n_ens):
        dv_arrival(k)
    vout_ref[...] = base[...] + TIME_STEP * (dv[0] + dv[1] + dv[2] + dv[3])

    for k in range(1, n_ens):
        dv_copy(k).wait_send()

    def sent(i, carry):
        for g in range(2):
            for r in range(2):
                pltpu.make_async_copy(sendbuf.at[g, i, r], sendbuf.at[g, i, r], ssem.at[g, i, r]).wait()
                told = labsend.at[g, i + 1, r]
                pltpu.make_async_copy(told, told, lssem.at[g, i + 1, r]).wait()
        return carry

    lax.fori_loop(0, 15, sent, 0)
    for g in range(2):
        pltpu.make_async_copy(sendbuf.at[g, 15, 1], sendbuf.at[g, 15, 1], ssem.at[g, 15, 1]).wait()
        pltpu.make_async_copy(labsend.at[g, 0, 1], labsend.at[g, 0, 1], lssem.at[g, 0, 1]).wait()


def on_device(conformations, fill_counts, dest_slots, dest_cells, velocity, noise):
    _, groups, blocks, slots = conformations.shape
    vmem = pl.BlockSpec(memory_space=pltpu.VMEM)
    hbm = pl.BlockSpec(memory_space=pl.ANY)
    tile = velocity.shape
    arguments = (conformations, fill_counts, dest_slots, dest_cells, velocity, noise)
    dma = pltpu.SemaphoreType.DMA
    return pl.pallas_call(
        kernel,
        out_shape=(
            pltpu.VMEM(noise.shape, F32),
            pltpu.VMEM(velocity.shape, F32),
        ),
        in_specs=[hbm] * 6,
        out_specs=(vmem, vmem),
        scratch_shapes=[
            pltpu.VMEM(conformations.shape, F32),
            pltpu.VMEM(fill_counts.shape, jnp.int32),
            pltpu.VMEM(fill_counts.shape, jnp.int32),
            pltpu.VMEM(fill_counts.shape, jnp.int32),
            pltpu.VMEM(tile, F32),
            pltpu.VMEM(noise.shape, F32),
            pltpu.VMEM((groups, blocks, 3 * slots), BF16),
            pltpu.VMEM((groups, blocks, 3 * slots), BF16),
            pltpu.VMEM((groups, 16, 2, 3, CAP, slots), F32),
            pltpu.VMEM((groups, 16, 2, 3, CAP, slots), F32),
            pltpu.VMEM((groups, 8, blocks), F32),
            pltpu.VMEM((groups, 16, 2, 4, 128), F32),
            pltpu.VMEM((groups, 16, 2, 4, 128), F32),
            pltpu.VMEM((groups, 16, 128, 16), F32),
            pltpu.VMEM((4,) + tile, F32),
            pltpu.VMEM((288, 128), BF16),
            pltpu.VMEM((4, 16, 128), F32),
            pltpu.VMEM((192, 128), F32),
            pltpu.VMEM(tile, F32),
            pltpu.VMEM(tile, F32),
            pltpu.VMEM((2,) + tile, F32),
            pltpu.VMEM((2,) + tile, F32),
            pltpu.VMEM((4,) + tile, F32),
            pltpu.VMEM(tile, F32),
            dma((2,)), dma((4,)), dma,
            dma((groups, 16, 2)), dma((groups, 16, 2)),
            dma((groups, 16, 2)), dma((groups, 16, 2)),
            dma((4,)), dma((4,)), dma((4,)), dma((4,)), dma((4,)), dma((4,)),
        ],
        compiler_params=pltpu.CompilerParams(
            collective_id=0, has_side_effects=True, vmem_limit_bytes=40 * 2**20
        ),
    )(*(pltpu.with_memory_space_constraint(x, pltpu.HBM) for x in arguments))


def solution(mesh):
    placed = (
        P(None, "ens", ("cx", "cy"), None),
        P("ens", ("cx", "cy")),
        P("ens", ("cx", "cy")),
        P("ens", ("cx", "cy")),
        P(None, "cx", "cy"),
        P(None, "ens", ("cx", "cy"), None),
    )
    return jax.shard_map(
        on_device,
        mesh=mesh,
        in_specs=placed,
        out_specs=(P(None, "ens", ("cx", "cy"), None), P(None, "cx", "cy")),
        check_vma=False,
    )
```

```python
import functools
import math

import jax
import jax.numpy as jnp
from jax import lax
from jax.experimental import pallas as pl
from jax.experimental.pallas import tpu as pltpu
from jax.sharding import PartitionSpec as P

DUMB = 64
NZ = 64
CAP = 48
TIME_STEP = 0.02
WEISSENBERG = 0.5
EXTENSION = 50.0
VISCOSITY = 1.0

PAIRS = ((0, 0), (1, 1), (2, 2), (0, 1), (0, 2), (1, 2))
ALONG_X = (0, 3, 4)
ALONG_Y = (3, 1, 5)
ALONG_Z = (4, 5, 2)

MESH = pl.DeviceIdType.MESH
F32 = jnp.float32
BF16 = jnp.bfloat16

OFFSETS = (
    (2, 2), (2, 1), (1, 2), (2, 3), (3, 2), (2, 0), (0, 2), (1, 1),
    (3, 3), (1, 3), (3, 1), (1, 0), (3, 0), (0, 1), (0, 3),
)
CODE_X = sum(dx * 4**i for i, (dx, _) in enumerate(OFFSETS))
CODE_Z = sum(dz * 4**i for i, (_, dz) in enumerate(OFFSETS))
HALVES = 2
PART = CAP // HALVES
NT = (((1,), (1,)), ((), ()))


def halves_of(values):
    high = values.astype(BF16)
    return high, (values - high.astype(F32)).astype(BF16)


def stencil(field, west, east, south, north):
    row = lax.broadcasted_iota(jnp.int32, field.shape, 0)
    lane = lax.broadcasted_iota(jnp.int32, field.shape, 1)
    rows, width = field.shape
    east_side = jnp.where(row == rows - 1, pltpu.roll(east, rows - 1, 0), pltpu.roll(field, rows - 1, 0))
    west_side = jnp.where(row == 0, pltpu.roll(west, 1, 0), pltpu.roll(field, 1, 0))
    north_side = jnp.where(
        lane >= width - NZ, pltpu.roll(north, width - NZ, 1), pltpu.roll(field, width - NZ, 1)
    )
    south_side = jnp.where(lane < NZ, pltpu.roll(south, NZ, 1), pltpu.roll(field, NZ, 1))
    return east_side, west_side, north_side, south_side


def along_z(field):
    lane = lax.rem(lax.broadcasted_iota(jnp.int32, field.shape, 1), NZ)
    width = field.shape[1]
    upper = jnp.where(lane < NZ - 1, pltpu.roll(field, width - 1, 1), 0.0)
    lower = jnp.where(lane > 0, pltpu.roll(field, 1, 1), 0.0)
    return upper, lower


def kernel(
    conf_hbm, fill_hbm, dest_hbm, cell_hbm, vel_hbm, noise_hbm,
    out_ref, vout_ref,
    conf, fill_ref, dest_ref, cell_ref, vel_ref, noise, high, low, sendbuf, recv, labels, labsend, labrecv, columns,
    vhalo, table, rowbuf, field, sx, sy, shx, shy, dv, base,
    conf_sem, in_sem, noise_sem, ssem, rsem, lssem, lrsem, vs_sem, vr_sem, hs_sem, hr_sem, ds_sem, dr_sem,
):
    ens = lax.axis_index("ens")
    cx = lax.axis_index("cx")
    cy = lax.axis_index("cy")
    my_x = lax.div(cx, 2)
    core = lax.rem(cx, 2)
    n_ens = 4

    def conf_copy(g):
        return pltpu.make_async_copy(conf_hbm.at[:, g], conf.at[:, g], conf_sem.at[g])

    small = [
        pltpu.make_async_copy(source, target, in_sem.at[k])
        for k, (source, target) in enumerate(
            ((dest_hbm, dest_ref), (vel_hbm, vel_ref), (fill_hbm, fill_ref), (cell_hbm, cell_ref))
        )
    ]
    conf_copy(0).start()
    for copy in small:
        copy.start()
    noise_copy = pltpu.make_async_copy(noise_hbm, noise, noise_sem)

    east_id = (ens, lax.rem(cx + 1, 8), cy)
    west_id = (ens, lax.rem(cx + 7, 8), cy)
    north_id = (ens, cx, lax.rem(cy + 1, 4))
    south_id = (ens, cx, lax.rem(cy + 3, 4))

    def chip(dx, dz, r):
        return (ens, lax.rem(my_x + dx, 4) * 2 + lax.rem(core + r, 2), lax.rem(cy + dz, 4))

    barrier = pltpu.get_barrier_semaphore()
    for dx, dz in OFFSETS:
        for r in range(2):
            pl.semaphore_signal(barrier, inc=1, device_id=chip(dx, dz, r), device_id_type=MESH)
    pl.semaphore_signal(barrier, inc=1, device_id=chip(0, 0, 1), device_id_type=MESH)
    for k in range(1, n_ens):
        pl.semaphore_signal(
            barrier, inc=1, device_id=(lax.rem(ens + k, n_ens), cx, cy), device_id_type=MESH
        )

    def split(g):
        for a in range(3):
            first, second = halves_of(conf[a, g])
            high[g, :, a * 128 : (a + 1) * 128] = first
            low[g, :, a * 128 : (a + 1) * 128] = second

    blocks = conf.shape[2]
    row48 = lax.broadcasted_iota(jnp.int32, (CAP, blocks), 0)
    lane128 = lax.broadcasted_iota(jnp.int32, (1, 128), 1)

    field[...] = jnp.zeros_like(field)
    rowbuf[...] = jnp.zeros_like(rowbuf)
    conf_copy(0).wait()
    conf_copy(1).start()
    split(0)
    for copy in small:
        copy.wait()
    pl.semaphore_wait(barrier, 31 + n_ens - 1)

    def vel_copy(slot, target):
        return pltpu.make_async_remote_copy(
            src_ref=vel_ref, dst_ref=vhalo.at[slot], send_sem=vs_sem.at[slot], recv_sem=vr_sem.at[slot],
            device_id=target, device_id_type=MESH,
        )

    halo_targets = (east_id, west_id, north_id, south_id)
    for slot in range(4):
        vel_copy(slot, halo_targets[slot]).start()

    def data_copy(g, i, p, r, h, target):
        rows = pl.ds(h * PART, PART)
        return pltpu.make_async_remote_copy(
            src_ref=sendbuf.at[g, i, r, :, rows], dst_ref=recv.at[g, p, r, :, rows],
            send_sem=ssem.at[g, i, r], recv_sem=rsem.at[g, p, r],
            device_id=target, device_id_type=MESH,
        )

    def label_copy(p, r, target):
        return pltpu.make_async_remote_copy(
            src_ref=labsend.at[p, r], dst_ref=labrecv.at[p, r],
            send_sem=lssem.at[p, r], recv_sem=lrsem.at[p, r],
            device_id=target, device_id_type=MESH,
        )

    def pack_batch(q, carry, g, width):
        code_x, code_z = carry
        targets, landing = [], []
        for _ in range(width):
            dx, dz = lax.rem(code_x, 4), lax.rem(code_z, 4)
            code_x, code_z = lax.div(code_x, 4), lax.div(code_z, 4)
            dx = jnp.where(core == 0, dx, lax.rem(4 - dx, 4))
            dz = jnp.where(core == 0, dz, lax.rem(4 - dz, 4))
            landing.append(dx * 4 + dz)
            targets += [chip(dx, dz, 0), chip(dx, dz, 1)]
        dest = dest_ref[g : g + 1, :]
        onehot = jnp.concatenate(
            [
                jnp.where(dest - (target[1] * 4 + target[2]) * CAP == row48, 1.0, 0.0).astype(BF16)
                for target in targets
            ],
            axis=0,
        )
        packed = jnp.dot(onehot, high[g], preferred_element_type=F32) + jnp.dot(
            onehot, low[g], preferred_element_type=F32
        )
        for n in range(2 * width):
            for a in range(3):
                sendbuf[g, width * q + n // 2, n % 2, a] = packed[
                    n * CAP : (n + 1) * CAP, a * 128 : (a + 1) * 128
                ]

        def start(first, last):
            for h in range(HALVES):
                for n in range(first, last):
                    data_copy(g, width * q + n // 2, landing[n // 2], n % 2, h, targets[n]).start()

        start(0, 2 * width - 2)

        @pl.when(q < 16 // width - 1)
        def _():
            start(2 * width - 2, 2 * width)

        @pl.when(q == 16 // width - 1)
        def _():
            start(2 * width - 1, 2 * width)
            pltpu.make_async_copy(sendbuf.at[g, 15, 0], recv.at[g, 0, 0], rsem.at[g, 0, 0]).start()

        return code_x, code_z

    codes = (jnp.int32(CODE_X), jnp.int32(CODE_Z))

    def send_blocks(g, first, last, width=4):
        start = tuple(jnp.int32(code // 4 ** (width * first)) for code in (CODE_X, CODE_Z))
        lax.fori_loop(first, last, functools.partial(pack_batch, g=g, width=width), start)

    send_blocks(0, 0, 2, width=2)
    send_blocks(0, 1, 2)

    lab_row = lax.broadcasted_iota(jnp.int32, (8, 128), 0)
    block_lane = lax.broadcasted_iota(jnp.int32, (128, 128), 1)

    def label_rows(k, carry, g):
        rows = pl.ds(pl.multiple_of(k * 128, 128), 128)
        fill = fill_ref[g : g + 1, rows]
        cell = cell_ref[g : g + 1, rows].astype(F32)
        live = block_lane < jnp.broadcast_to(fill, (8, 128)).T[:, 0:1]
        fill = fill.astype(F32)
        x = [jnp.where(live, conf[a, g, rows], 0.0) for a in range(3)]
        inverse = 1.0 / (1.0 - (x[0] * x[0] + x[1] * x[1] + x[2] * x[2]) / EXTENSION)
        spring = [x[a] * inverse for a in range(3)]
        sums = jnp.zeros((128, 128), F32)
        for c, (a, b) in enumerate(PAIRS):
            sums = jnp.where(block_lane == c + 2, jnp.sum(x[a] * spring[b], axis=1, keepdims=True), sums)
        sums = sums.T[:8]
        labels[g, :, rows] = jnp.where(lab_row == 0, fill, jnp.where(lab_row == 1, cell, sums))
        return carry

    conf_copy(1).wait()
    noise_copy.start()
    for g in range(2):
        lax.fori_loop(0, blocks // 128, functools.partial(label_rows, g=g), 0)

    row128 = lax.broadcasted_iota(jnp.int32, (128, blocks), 0)

    def send_labels():
        told = jnp.zeros((256, 128), F32)
        for g in range(2):
            dest = dest_ref[g : g + 1, :]
            owner = ((dest.astype(F32) + 0.5) * (1.0 / CAP)).astype(jnp.int32)
            slot = dest - owner * CAP
            where_to = jnp.where(row128 - 64 * g == slot, 1.0, 0.0).astype(BF16)
            values = labels[g]
            first = values.astype(BF16).astype(F32)
            masks = []
            for p in range(16):
                for r in range(2):
                    _, x, z = chip(p // 4, p % 4, r)
                    masks.append(jnp.broadcast_to(owner == x * 4 + z, values.shape))
            for term in (first, values - first):
                spread = jnp.concatenate(
                    [
                        jnp.concatenate(
                            [jnp.where(masks[n], term, 0.0), jnp.where(masks[n + 1], term, 0.0)], axis=0
                        ).astype(BF16)
                        for n in range(0, 32, 2)
                    ],
                    axis=0,
                )
                told = told + lax.dot_general(spread, where_to, NT, preferred_element_type=F32)
        for p in range(16):
            for r in range(2):
                labsend[p, r] = told[16 * p + 8 * r : 16 * p + 8 * r + 8]
        label_copy(0, 1, chip(0, 0, 1)).start()
        pltpu.make_async_copy(labsend.at[0, 0], labrecv.at[0, 0], lrsem.at[0, 0]).start()

        def start(p, carry):
            for r in range(2):
                label_copy(p, r, chip(lax.div(p, 4), lax.rem(p, 4), r)).start()
            return carry

        lax.fori_loop(1, 16, start, 0)

    send_labels()

    send_blocks(0, 2, 4)
    split(1)
    send_blocks(1, 0, 2)

    for slot in range(4):
        vel_copy(slot, halo_targets[slot]).wait()
    inside = (cx > 0, cx < 7, cy > 0, cy < 3)

    def masked(tile, k):
        return jnp.where(inside[k], tile, 0.0)

    for a in range(3):
        f = vel_ref[a]
        e, w, n, s = stencil(f, *(masked(vhalo[k, a], k) for k in range(4)))
        u, d = along_z(f)
        base[a] = f + TIME_STEP * VISCOSITY * (e + w + n + s + u + d - 6.0 * f)
        for b, slope in enumerate((0.5 * (e - w), 0.5 * (n - s), 0.5 * (u - d))):
            first, second = halves_of(jnp.concatenate([slope[:, :128], slope[:, 128:]], axis=0))
            top = (3 * a + b) * 16
            table[top : top + 16] = first
            table[144 + top : 144 + top + 16] = second

    square = lax.broadcasted_iota(jnp.int32, (128, 128), 0)
    row_hi = lax.broadcasted_iota(jnp.int32, (16, 128), 0)

    def read_labels(q, carry, g):
        told, lows, highs = [], [], []
        for m in range(4):
            p = 4 * q + m
            if g == 0:
                for r in range(2):
                    pltpu.make_async_copy(labrecv.at[p, r], labrecv.at[p, r], lrsem.at[p, r]).wait()
            lab0, lab1 = labrecv[p, 0], labrecv[p, 1]
            if g == 0:
                here = jnp.where(lane128 < 64, lab0, pltpu.roll(lab1, 64, 1))
            else:
                here = jnp.where(lane128 < 64, pltpu.roll(lab0, 64, 1), lab1)
            cells = here[1:2].astype(jnp.int32)
            cell_hi = lax.div(cells, 128)
            cell_hi = lax.rem(cell_hi, 2) * 8 + lax.div(cell_hi, 2)
            told.append(here)
            lows.append(jnp.where(square == lax.rem(cells, 128), 1.0, 0.0).astype(BF16))
            highs.append(jnp.where(row_hi == cell_hi, 1.0, 0.0))
        at_lo = jnp.concatenate(lows, axis=1)
        spread = jnp.concatenate(
            [jnp.concatenate([told[m][c + 2 : c + 3] * highs[m] for c in range(6)], axis=0) for m in range(4)], axis=1
        )
        first, second = halves_of(spread)
        field[...] += lax.dot_general(
            jnp.concatenate([first, second], axis=0), at_lo, NT, preferred_element_type=F32
        )
        looked = jnp.dot(table[...], at_lo, preferred_element_type=F32)
        looked = looked[:144] + looked[144:]
        for m in range(4):
            for c in range(9):
                rowbuf[m, c : c + 1] = jnp.sum(
                    looked[16 * c : 16 * c + 16, 128 * m : 128 * m + 128] * highs[m], axis=0, keepdims=True
                )
            rowbuf[m, 9:10] = told[m][0:1]
        for m in range(4):
            columns[g, 4 * q + m] = rowbuf[m].T
        return carry

    for g in range(2):
        lax.fori_loop(0, 4, functools.partial(read_labels, g=g), 0)

    total = (field[:96] + field[96:]) / (WEISSENBERG * DUMB)
    stress = [
        jnp.concatenate([total[16 * c : 16 * c + 8], total[16 * c + 8 : 16 * c + 16]], axis=1) for c in range(6)
    ]
    for k in range(3):
        sx[k] = stress[ALONG_X[k]]
        sy[k] = stress[ALONG_Y[k]]
        u, d = along_z(stress[ALONG_Z[k]])
        dv[ens, k] = 0.5 * (u - d)

    def stress_copy(slot):
        return pltpu.make_async_remote_copy(
            src_ref=sx if slot < 2 else sy, dst_ref=shx.at[slot] if slot < 2 else shy.at[slot - 2],
            send_sem=hs_sem.at[slot], recv_sem=hr_sem.at[slot],
            device_id=halo_targets[slot], device_id_type=MESH,
        )

    for slot in range(4):
        stress_copy(slot).start()

    send_blocks(1, 2, 4)
    noise_copy.wait()
    slot_lane = lax.broadcasted_iota(jnp.int32, (CAP, 128), 1).astype(F32)

    def arrive(j, carry, g):
        code_x, code_z = carry
        own = j == 0
        i = lax.rem(j + 15, 16)
        dx = jnp.where(own, 0, lax.rem(code_x, 4))
        dz = jnp.where(own, 0, lax.rem(code_z, 4))
        code_x = jnp.where(own, code_x, lax.div(code_x, 4))
        code_z = jnp.where(own, code_z, lax.div(code_z, 4))
        def sent(r):
            pltpu.make_async_copy(sendbuf.at[g, i, r], sendbuf.at[g, i, r], ssem.at[g, i, r]).wait()
            if g == 0:
                pltpu.make_async_copy(labsend.at[j, r], labsend.at[j, r], lssem.at[j, r]).wait()

        pl.when(j > 0)(lambda: sent(0))
        sent(1)
        for r in range(2):
            landed = recv.at[g, dx * 4 + dz, r]
            pltpu.make_async_copy(landed, landed, rsem.at[g, dx * 4 + dz, r]).wait()
        for r in range(2):
            source = (lax.rem(my_x + 4 - dx, 4) * 2 + lax.rem(core + r, 2)) * 4 + lax.rem(cy + 4 - dz, 4)
            rows = pl.ds(pl.multiple_of(source * CAP, CAP), CAP)
            here = columns[g, dx * 4 + dz, r * 64 : r * 64 + CAP]
            live = slot_lane < here[:, 9:10]
            x = [jnp.where(live, recv[g, dx * 4 + dz, r, a], 0.0) for a in range(3)]
            inverse = 1.0 / (1.0 - (x[0] * x[0] + x[1] * x[1] + x[2] * x[2]) / EXTENSION)
            for a in range(3):
                stretch = sum(here[:, 3 * a + b : 3 * a + b + 1] * x[b] for b in range(3))
                stepped = (
                    x[a]
                    + TIME_STEP * (stretch - x[a] * inverse / (2.0 * WEISSENBERG))
                    + math.sqrt(TIME_STEP / WEISSENBERG) * noise[a, g, rows]
                )
                out_ref[a, g, rows] = jnp.where(live, stepped, 0.0)
        return code_x, code_z

    lax.fori_loop(0, 16, functools.partial(arrive, g=0), codes)
    for slot in range(4):
        stress_copy(slot).wait()
    for k in range(3):
        fx, fy = sx[k], sy[k]
        e, w, _, _ = stencil(fx, masked(shx[0, k], 0), masked(shx[1, k], 1), fx, fx)
        _, _, n, s = stencil(fy, fy, fy, masked(shy[0, k], 2), masked(shy[1, k], 3))
        dv[ens, k] = dv[ens, k] + 0.5 * (e - w) + 0.5 * (n - s)

    def dv_copy(k):
        return pltpu.make_async_remote_copy(
            src_ref=dv.at[ens], dst_ref=dv.at[ens], send_sem=ds_sem.at[k], recv_sem=dr_sem.at[k],
            device_id=(lax.rem(ens + k, n_ens), cx, cy), device_id_type=MESH,
        )

    def dv_arrival(k):
        source = lax.rem(ens + n_ens - k, n_ens)
        pltpu.make_async_copy(dv.at[source], dv.at[source], dr_sem.at[k]).wait()

    for k in range(1, n_ens):
        dv_copy(k).start()


    lax.fori_loop(0, 16, functools.partial(arrive, g=1), codes)

    for k in range(1, n_ens):
        dv_arrival(k)
    vout_ref[...] = base[...] + TIME_STEP * (dv[0] + dv[1] + dv[2] + dv[3])

    for k in range(1, n_ens):
        dv_copy(k).wait_send()


def finish(conf_vmem, velocity_vmem, conf_hbm, velocity_hbm, sems):
    copies = [pltpu.make_async_copy(velocity_vmem, velocity_hbm, sems.at[6])]
    for a in range(3):
        for g in range(2):
            copies.append(pltpu.make_async_copy(conf_vmem.at[a, g], conf_hbm.at[a, g], sems.at[2 * a + g]))
    for copy in copies:
        copy.start()
    for copy in copies:
        copy.wait()


def on_device(conformations, fill_counts, dest_slots, dest_cells, velocity, noise):
    _, groups, blocks, slots = conformations.shape
    vmem = pl.BlockSpec(memory_space=pltpu.VMEM)
    hbm = pl.BlockSpec(memory_space=pl.ANY)
    tile = velocity.shape
    arguments = (conformations, fill_counts, dest_slots, dest_cells, velocity, noise)
    dma = pltpu.SemaphoreType.DMA
    results = pl.pallas_call(
        kernel,
        out_shape=(
            pltpu.VMEM(noise.shape, F32),
            pltpu.VMEM(velocity.shape, F32),
        ),
        in_specs=[hbm] * 6,
        out_specs=(vmem, vmem),
        scratch_shapes=[
            pltpu.VMEM(conformations.shape, F32),
            pltpu.VMEM(fill_counts.shape, jnp.int32),
            pltpu.VMEM(fill_counts.shape, jnp.int32),
            pltpu.VMEM(fill_counts.shape, jnp.int32),
            pltpu.VMEM(tile, F32),
            pltpu.VMEM(noise.shape, F32),
            pltpu.VMEM((groups, blocks, 3 * slots), BF16),
            pltpu.VMEM((groups, blocks, 3 * slots), BF16),
            pltpu.VMEM((groups, 16, 2, 3, CAP, slots), F32),
            pltpu.VMEM((groups, 16, 2, 3, CAP, slots), F32),
            pltpu.VMEM((groups, 8, blocks), F32),
            pltpu.VMEM((16, 2, 8, 128), F32),
            pltpu.VMEM((16, 2, 8, 128), F32),
            pltpu.VMEM((groups, 16, 128, 16), F32),
            pltpu.VMEM((4,) + tile, F32),
            pltpu.VMEM((288, 128), BF16),
            pltpu.VMEM((4, 16, 128), F32),
            pltpu.VMEM((192, 128), F32),
            pltpu.VMEM(tile, F32),
            pltpu.VMEM(tile, F32),
            pltpu.VMEM((2,) + tile, F32),
            pltpu.VMEM((2,) + tile, F32),
            pltpu.VMEM((4,) + tile, F32),
            pltpu.VMEM(tile, F32),
            dma((2,)), dma((4,)), dma,
            dma((groups, 16, 2)), dma((groups, 16, 2)), dma((16, 2)), dma((16, 2)),
            dma((4,)), dma((4,)), dma((4,)), dma((4,)), dma((4,)), dma((4,)),
        ],
        compiler_params=pltpu.CompilerParams(
            collective_id=0, has_side_effects=True, vmem_limit_bytes=40 * 2**20
        ),
    )(*(pltpu.with_memory_space_constraint(x, pltpu.HBM) for x in arguments))
    return pl.pallas_call(
        finish,
        out_shape=tuple(jax.ShapeDtypeStruct(x.shape, F32) for x in results),
        in_specs=[vmem, vmem],
        out_specs=(hbm, hbm),
        scratch_shapes=[dma((7,))],
        compiler_params=pltpu.CompilerParams(vmem_limit_bytes=2**20),
    )(*(pltpu.with_memory_space_constraint(x, pltpu.VMEM) for x in results))


def solution(mesh):
    placed = (
        P(None, "ens", ("cx", "cy"), None),
        P("ens", ("cx", "cy")),
        P("ens", ("cx", "cy")),
        P("ens", ("cx", "cy")),
        P(None, "cx", "cy"),
        P(None, "ens", ("cx", "cy"), None),
    )
    return jax.shard_map(
        on_device,
        mesh=mesh,
        in_specs=placed,
        out_specs=(P(None, "ens", ("cx", "cy"), None), P(None, "cx", "cy")),
        check_vma=False,
    )
```

```python
import functools
import math

import jax
import jax.numpy as jnp
from jax import lax
from jax.experimental import pallas as pl
from jax.experimental.pallas import tpu as pltpu
from jax.sharding import PartitionSpec as P

DUMB = 64
NZ = 64
CAP = 48
TIME_STEP = 0.02
WEISSENBERG = 0.5
EXTENSION = 50.0
VISCOSITY = 1.0

PAIRS = ((0, 0), (1, 1), (2, 2), (0, 1), (0, 2), (1, 2))
ALONG_X = (0, 3, 4)
ALONG_Y = (3, 1, 5)
ALONG_Z = (4, 5, 2)

MESH = pl.DeviceIdType.MESH
F32 = jnp.float32
BF16 = jnp.bfloat16

OFFSETS = (
    (2, 2), (2, 1), (1, 2), (2, 3), (3, 2), (2, 0), (0, 2), (1, 1),
    (3, 3), (1, 3), (3, 1), (1, 0), (3, 0), (0, 1), (0, 3),
)
CODE_X = sum(dx * 4**i for i, (dx, _) in enumerate(OFFSETS))
CODE_Z = sum(dz * 4**i for i, (_, dz) in enumerate(OFFSETS))
HALVES = 2
PART = CAP // HALVES
NT = (((1,), (1,)), ((), ()))


def halves_of(values):
    high = values.astype(BF16)
    return high, (values - high.astype(F32)).astype(BF16)


def stencil(field, west, east, south, north):
    row = lax.broadcasted_iota(jnp.int32, field.shape, 0)
    lane = lax.broadcasted_iota(jnp.int32, field.shape, 1)
    rows, width = field.shape
    east_side = jnp.where(row == rows - 1, pltpu.roll(east, rows - 1, 0), pltpu.roll(field, rows - 1, 0))
    west_side = jnp.where(row == 0, pltpu.roll(west, 1, 0), pltpu.roll(field, 1, 0))
    north_side = jnp.where(
        lane >= width - NZ, pltpu.roll(north, width - NZ, 1), pltpu.roll(field, width - NZ, 1)
    )
    south_side = jnp.where(lane < NZ, pltpu.roll(south, NZ, 1), pltpu.roll(field, NZ, 1))
    return east_side, west_side, north_side, south_side


def along_z(field):
    lane = lax.rem(lax.broadcasted_iota(jnp.int32, field.shape, 1), NZ)
    width = field.shape[1]
    upper = jnp.where(lane < NZ - 1, pltpu.roll(field, width - 1, 1), 0.0)
    lower = jnp.where(lane > 0, pltpu.roll(field, 1, 1), 0.0)
    return upper, lower


def kernel(
    conf_hbm, fill_hbm, dest_hbm, cell_hbm, vel_hbm, noise_hbm,
    out_ref, vout_ref,
    conf, fill_ref, dest_ref, cell_ref, vel_ref, noise, high, low, sendbuf, recv, labels, labsend, labrecv, columns,
    vhalo, table, rowbuf, field, sx, sy, shx, shy, dv, base,
    conf_sem, in_sem, noise_sem, ssem, rsem, lssem, lrsem, vs_sem, vr_sem, hs_sem, hr_sem, ds_sem, dr_sem,
):
    ens = lax.axis_index("ens")
    cx = lax.axis_index("cx")
    cy = lax.axis_index("cy")
    my_x = lax.div(cx, 2)
    core = lax.rem(cx, 2)
    n_ens = 4

    def conf_copy(g):
        return pltpu.make_async_copy(conf_hbm.at[:, g], conf.at[:, g], conf_sem.at[g])

    small = [
        pltpu.make_async_copy(source, target, in_sem.at[k])
        for k, (source, target) in enumerate(
            ((dest_hbm, dest_ref), (vel_hbm, vel_ref), (fill_hbm, fill_ref), (cell_hbm, cell_ref))
        )
    ]
    conf_copy(0).start()
    for copy in small:
        copy.start()
    noise_copy = pltpu.make_async_copy(noise_hbm, noise, noise_sem)

    east_id = (ens, lax.rem(cx + 1, 8), cy)
    west_id = (ens, lax.rem(cx + 7, 8), cy)
    north_id = (ens, cx, lax.rem(cy + 1, 4))
    south_id = (ens, cx, lax.rem(cy + 3, 4))

    def chip(dx, dz, r):
        return (ens, lax.rem(my_x + dx, 4) * 2 + lax.rem(core + r, 2), lax.rem(cy + dz, 4))

    barrier = pltpu.get_barrier_semaphore()
    for dx, dz in OFFSETS:
        for r in range(2):
            pl.semaphore_signal(barrier, inc=1, device_id=chip(dx, dz, r), device_id_type=MESH)
    pl.semaphore_signal(barrier, inc=1, device_id=chip(0, 0, 1), device_id_type=MESH)
    for k in range(1, n_ens):
        pl.semaphore_signal(
            barrier, inc=1, device_id=(lax.rem(ens + k, n_ens), cx, cy), device_id_type=MESH
        )

    def split(g):
        for a in range(3):
            first, second = halves_of(conf[a, g])
            high[g, :, a * 128 : (a + 1) * 128] = first
            low[g, :, a * 128 : (a + 1) * 128] = second

    blocks = conf.shape[2]
    row48 = lax.broadcasted_iota(jnp.int32, (CAP, blocks), 0)
    lane128 = lax.broadcasted_iota(jnp.int32, (1, 128), 1)

    field[...] = jnp.zeros_like(field)
    rowbuf[...] = jnp.zeros_like(rowbuf)
    conf_copy(0).wait()
    conf_copy(1).start()
    split(0)
    for copy in small:
        copy.wait()

    def vel_copy(slot, target):
        return pltpu.make_async_remote_copy(
            src_ref=vel_ref, dst_ref=vhalo.at[slot], send_sem=vs_sem.at[slot], recv_sem=vr_sem.at[slot],
            device_id=target, device_id_type=MESH,
        )

    halo_targets = (east_id, west_id, north_id, south_id)

    def data_copy(g, i, p, r, h, target):
        return pltpu.make_async_remote_copy(
            src_ref=sendbuf.at[g, i, r, h], dst_ref=recv.at[g, p, r, h],
            send_sem=ssem.at[g, i, r], recv_sem=rsem.at[g, p, r],
            device_id=target, device_id_type=MESH,
        )

    def label_copy(p, r, target):
        return pltpu.make_async_remote_copy(
            src_ref=labsend.at[p, r], dst_ref=labrecv.at[p, r],
            send_sem=lssem.at[p, r], recv_sem=lrsem.at[p, r],
            device_id=target, device_id_type=MESH,
        )

    def pack_batch(q, carry, g, width, mode=3):
        code_x, code_z = carry
        targets, landing = [], []
        for _ in range(width):
            dx, dz = lax.rem(code_x, 4), lax.rem(code_z, 4)
            code_x, code_z = lax.div(code_x, 4), lax.div(code_z, 4)
            dx = jnp.where(core == 0, dx, lax.rem(4 - dx, 4))
            dz = jnp.where(core == 0, dz, lax.rem(4 - dz, 4))
            landing.append(dx * 4 + dz)
            targets += [chip(dx, dz, 0), chip(dx, dz, 1)]
        if mode & 1:
            fill_batch(q, g, width, targets)
        if mode & 2:
            start_batch(q, g, width, targets, landing)
        return code_x, code_z

    def fill_batch(q, g, width, targets):
        dest = dest_ref[g : g + 1, :]
        onehot = jnp.concatenate(
            [
                jnp.where(dest - (target[1] * 4 + target[2]) * CAP == row48, 1.0, 0.0).astype(BF16)
                for target in targets
            ],
            axis=0,
        )
        packed = jnp.dot(onehot, high[g], preferred_element_type=F32) + jnp.dot(
            onehot, low[g], preferred_element_type=F32
        )
        for n in range(2 * width):
            for h in range(HALVES):
                for a in range(3):
                    sendbuf[g, width * q + n // 2, n % 2, h, a] = packed[
                        n * CAP + h * PART : n * CAP + (h + 1) * PART, a * 128 : (a + 1) * 128
                    ]

    def start_batch(q, g, width, targets, landing):
        def start(first, last):
            for h in range(HALVES):
                for n in range(first, last):
                    data_copy(g, width * q + n // 2, landing[n // 2], n % 2, h, targets[n]).start()

        start(0, 2 * width - 2)

        @pl.when(q < 16 // width - 1)
        def _():
            start(2 * width - 2, 2 * width)

        @pl.when(q == 16 // width - 1)
        def _():
            start(2 * width - 1, 2 * width)
            pltpu.make_async_copy(sendbuf.at[g, 15, 0], recv.at[g, 0, 0], rsem.at[g, 0, 0]).start()

    codes = (jnp.int32(CODE_X), jnp.int32(CODE_Z))

    def send_blocks(g, first, last, width=4, mode=3):
        start = tuple(jnp.int32(code // 4 ** (width * first)) for code in (CODE_X, CODE_Z))
        lax.fori_loop(first, last, functools.partial(pack_batch, g=g, width=width, mode=mode), start)

    send_blocks(0, 0, 2, mode=1)
    pl.semaphore_wait(barrier, 31 + n_ens - 1)
    for slot in range(4):
        vel_copy(slot, halo_targets[slot]).start()
    send_blocks(0, 0, 2, mode=2)

    lab_row = lax.broadcasted_iota(jnp.int32, (8, 128), 0)
    block_lane = lax.broadcasted_iota(jnp.int32, (128, 128), 1)

    def label_rows(k, carry, g):
        rows = pl.ds(pl.multiple_of(k * 128, 128), 128)
        fill = fill_ref[g : g + 1, rows]
        cell = cell_ref[g : g + 1, rows].astype(F32)
        live = block_lane < jnp.broadcast_to(fill, (8, 128)).T[:, 0:1]
        fill = fill.astype(F32)
        x = [jnp.where(live, conf[a, g, rows], 0.0) for a in range(3)]
        inverse = 1.0 / (1.0 - (x[0] * x[0] + x[1] * x[1] + x[2] * x[2]) / EXTENSION)
        spring = [x[a] * inverse for a in range(3)]
        sums = jnp.zeros((128, 128), F32)
        for c, (a, b) in enumerate(PAIRS):
            sums = jnp.where(block_lane == c + 2, jnp.sum(x[a] * spring[b], axis=1, keepdims=True), sums)
        sums = sums.T[:8]
        labels[g, :, rows] = jnp.where(lab_row == 0, fill, jnp.where(lab_row == 1, cell, sums))
        return carry

    conf_copy(1).wait()
    noise_copy.start()
    for g in range(2):
        lax.fori_loop(0, blocks // 128, functools.partial(label_rows, g=g), 0)

    row128 = lax.broadcasted_iota(jnp.int32, (128, blocks), 0)

    def send_labels():
        told = jnp.zeros((256, 128), F32)
        for g in range(2):
            dest = dest_ref[g : g + 1, :]
            owner = ((dest.astype(F32) + 0.5) * (1.0 / CAP)).astype(jnp.int32)
            slot = dest - owner * CAP
            where_to = jnp.where(row128 - 64 * g == slot, 1.0, 0.0).astype(BF16)
            values = labels[g]
            first = values.astype(BF16).astype(F32)
            masks = []
            for p in range(16):
                for r in range(2):
                    _, x, z = chip(p // 4, p % 4, r)
                    masks.append(jnp.broadcast_to(owner == x * 4 + z, values.shape))
            for term in (first, values - first):
                spread = jnp.concatenate(
                    [
                        jnp.concatenate(
                            [jnp.where(masks[n], term, 0.0), jnp.where(masks[n + 1], term, 0.0)], axis=0
                        ).astype(BF16)
                        for n in range(0, 32, 2)
                    ],
                    axis=0,
                )
                told = told + lax.dot_general(spread, where_to, NT, preferred_element_type=F32)
        for p in range(16):
            for r in range(2):
                labsend[p, r] = told[16 * p + 8 * r : 16 * p + 8 * r + 8]
        label_copy(0, 1, chip(0, 0, 1)).start()
        pltpu.make_async_copy(labsend.at[0, 0], labrecv.at[0, 0], lrsem.at[0, 0]).start()

        def start(p, carry):
            for r in range(2):
                label_copy(p, r, chip(lax.div(p, 4), lax.rem(p, 4), r)).start()
            return carry

        lax.fori_loop(1, 16, start, 0)

    send_labels()

    send_blocks(0, 2, 4)
    split(1)
    send_blocks(1, 0, 2)

    for slot in range(4):
        vel_copy(slot, halo_targets[slot]).wait()
    inside = (cx > 0, cx < 7, cy > 0, cy < 3)

    def masked(tile, k):
        return jnp.where(inside[k], tile, 0.0)

    for a in range(3):
        f = vel_ref[a]
        e, w, n, s = stencil(f, *(masked(vhalo[k, a], k) for k in range(4)))
        u, d = along_z(f)
        base[a] = f + TIME_STEP * VISCOSITY * (e + w + n + s + u + d - 6.0 * f)
        for b, slope in enumerate((0.5 * (e - w), 0.5 * (n - s), 0.5 * (u - d))):
            first, second = halves_of(jnp.concatenate([slope[:, :128], slope[:, 128:]], axis=0))
            top = (3 * a + b) * 16
            table[top : top + 16] = first
            table[144 + top : 144 + top + 16] = second

    square = lax.broadcasted_iota(jnp.int32, (128, 128), 0)
    row_hi = lax.broadcasted_iota(jnp.int32, (16, 128), 0)

    def read_labels(q, carry, g):
        told, lows, highs = [], [], []
        for m in range(4):
            p = 4 * q + m
            if g == 0:
                for r in range(2):
                    pltpu.make_async_copy(labrecv.at[p, r], labrecv.at[p, r], lrsem.at[p, r]).wait()
            lab0, lab1 = labrecv[p, 0], labrecv[p, 1]
            if g == 0:
                here = jnp.where(lane128 < 64, lab0, pltpu.roll(lab1, 64, 1))
            else:
                here = jnp.where(lane128 < 64, pltpu.roll(lab0, 64, 1), lab1)
            cells = here[1:2].astype(jnp.int32)
            cell_hi = lax.div(cells, 128)
            cell_hi = lax.rem(cell_hi, 2) * 8 + lax.div(cell_hi, 2)
            told.append(here)
            lows.append(jnp.where(square == lax.rem(cells, 128), 1.0, 0.0).astype(BF16))
            highs.append(jnp.where(row_hi == cell_hi, 1.0, 0.0))
        at_lo = jnp.concatenate(lows, axis=1)
        spread = jnp.concatenate(
            [jnp.concatenate([told[m][c + 2 : c + 3] * highs[m] for c in range(6)], axis=0) for m in range(4)], axis=1
        )
        first, second = halves_of(spread)
        field[...] += lax.dot_general(
            jnp.concatenate([first, second], axis=0), at_lo, NT, preferred_element_type=F32
        )
        looked = jnp.dot(table[...], at_lo, preferred_element_type=F32)
        looked = looked[:144] + looked[144:]
        for m in range(4):
            for c in range(9):
                rowbuf[m, c : c + 1] = jnp.sum(
                    looked[16 * c : 16 * c + 16, 128 * m : 128 * m + 128] * highs[m], axis=0, keepdims=True
                )
            rowbuf[m, 9:10] = told[m][0:1]
        for m in range(4):
            columns[g, 4 * q + m] = rowbuf[m].T
        return carry

    for g in range(2):
        lax.fori_loop(0, 4, functools.partial(read_labels, g=g), 0)

    total = (field[:96] + field[96:]) / (WEISSENBERG * DUMB)
    stress = [
        jnp.concatenate([total[16 * c : 16 * c + 8], total[16 * c + 8 : 16 * c + 16]], axis=1) for c in range(6)
    ]
    for k in range(3):
        sx[k] = stress[ALONG_X[k]]
        sy[k] = stress[ALONG_Y[k]]
        u, d = along_z(stress[ALONG_Z[k]])
        dv[ens, k] = 0.5 * (u - d)

    def stress_copy(slot):
        return pltpu.make_async_remote_copy(
            src_ref=sx if slot < 2 else sy, dst_ref=shx.at[slot] if slot < 2 else shy.at[slot - 2],
            send_sem=hs_sem.at[slot], recv_sem=hr_sem.at[slot],
            device_id=halo_targets[slot], device_id_type=MESH,
        )

    for slot in range(4):
        stress_copy(slot).start()

    send_blocks(1, 2, 4)
    noise_copy.wait()
    slot_lane = lax.broadcasted_iota(jnp.int32, (CAP, 128), 1).astype(F32)

    def arrive(j, carry, g):
        code_x, code_z = carry
        own = j == 0
        i = lax.rem(j + 15, 16)
        dx = jnp.where(own, 0, lax.rem(code_x, 4))
        dz = jnp.where(own, 0, lax.rem(code_z, 4))
        code_x = jnp.where(own, code_x, lax.div(code_x, 4))
        code_z = jnp.where(own, code_z, lax.div(code_z, 4))
        def sent(r):
            pltpu.make_async_copy(sendbuf.at[g, i, r], sendbuf.at[g, i, r], ssem.at[g, i, r]).wait()
            if g == 0:
                pltpu.make_async_copy(labsend.at[j, r], labsend.at[j, r], lssem.at[j, r]).wait()

        pl.when(j > 0)(lambda: sent(0))
        sent(1)
        for r in range(2):
            landed = recv.at[g, dx * 4 + dz, r]
            pltpu.make_async_copy(landed, landed, rsem.at[g, dx * 4 + dz, r]).wait()
        for r in range(2):
            source = (lax.rem(my_x + 4 - dx, 4) * 2 + lax.rem(core + r, 2)) * 4 + lax.rem(cy + 4 - dz, 4)
            rows = pl.ds(pl.multiple_of(source * CAP, CAP), CAP)
            here = columns[g, dx * 4 + dz, r * 64 : r * 64 + CAP]
            live = slot_lane < here[:, 9:10]
            x = [
                jnp.where(
                    live, jnp.concatenate([recv[g, dx * 4 + dz, r, h, a] for h in range(HALVES)], axis=0), 0.0
                )
                for a in range(3)
            ]
            inverse = 1.0 / (1.0 - (x[0] * x[0] + x[1] * x[1] + x[2] * x[2]) / EXTENSION)
            for a in range(3):
                stretch = sum(here[:, 3 * a + b : 3 * a + b + 1] * x[b] for b in range(3))
                stepped = (
                    x[a]
                    + TIME_STEP * (stretch - x[a] * inverse / (2.0 * WEISSENBERG))
                    + math.sqrt(TIME_STEP / WEISSENBERG) * noise[a, g, rows]
                )
                out_ref[a, g, rows] = jnp.where(live, stepped, 0.0)
        return code_x, code_z

    lax.fori_loop(0, 16, functools.partial(arrive, g=0), codes)
    for slot in range(4):
        stress_copy(slot).wait()
    for k in range(3):
        fx, fy = sx[k], sy[k]
        e, w, _, _ = stencil(fx, masked(shx[0, k], 0), masked(shx[1, k], 1), fx, fx)
        _, _, n, s = stencil(fy, fy, fy, masked(shy[0, k], 2), masked(shy[1, k], 3))
        dv[ens, k] = dv[ens, k] + 0.5 * (e - w) + 0.5 * (n - s)

    def dv_copy(k):
        return pltpu.make_async_remote_copy(
            src_ref=dv.at[ens], dst_ref=dv.at[ens], send_sem=ds_sem.at[k], recv_sem=dr_sem.at[k],
            device_id=(lax.rem(ens + k, n_ens), cx, cy), device_id_type=MESH,
        )

    def dv_arrival(k):
        source = lax.rem(ens + n_ens - k, n_ens)
        pltpu.make_async_copy(dv.at[source], dv.at[source], dr_sem.at[k]).wait()

    for k in range(1, n_ens):
        dv_copy(k).start()


    lax.fori_loop(0, 16, functools.partial(arrive, g=1), codes)

    for k in range(1, n_ens):
        dv_arrival(k)
    vout_ref[...] = base[...] + TIME_STEP * (dv[0] + dv[1] + dv[2] + dv[3])

    for k in range(1, n_ens):
        dv_copy(k).wait_send()


def finish(conf_vmem, velocity_vmem, conf_hbm, velocity_hbm, sems):
    copies = [pltpu.make_async_copy(velocity_vmem, velocity_hbm, sems.at[6])]
    for a in range(3):
        for g in range(2):
            copies.append(pltpu.make_async_copy(conf_vmem.at[a, g], conf_hbm.at[a, g], sems.at[2 * a + g]))
    for copy in copies:
        copy.start()
    for copy in copies:
        copy.wait()


def on_device(conformations, fill_counts, dest_slots, dest_cells, velocity, noise):
    _, groups, blocks, slots = conformations.shape
    vmem = pl.BlockSpec(memory_space=pltpu.VMEM)
    hbm = pl.BlockSpec(memory_space=pl.ANY)
    tile = velocity.shape
    arguments = (conformations, fill_counts, dest_slots, dest_cells, velocity, noise)
    dma = pltpu.SemaphoreType.DMA
    results = pl.pallas_call(
        kernel,
        out_shape=(
            pltpu.VMEM(noise.shape, F32),
            pltpu.VMEM(velocity.shape, F32),
        ),
        in_specs=[hbm] * 6,
        out_specs=(vmem, vmem),
        scratch_shapes=[
            pltpu.VMEM(conformations.shape, F32),
            pltpu.VMEM(fill_counts.shape, jnp.int32),
            pltpu.VMEM(fill_counts.shape, jnp.int32),
            pltpu.VMEM(fill_counts.shape, jnp.int32),
            pltpu.VMEM(tile, F32),
            pltpu.VMEM(noise.shape, F32),
            pltpu.VMEM((groups, blocks, 3 * slots), BF16),
            pltpu.VMEM((groups, blocks, 3 * slots), BF16),
            pltpu.VMEM((groups, 16, 2, HALVES, 3, PART, slots), F32),
            pltpu.VMEM((groups, 16, 2, HALVES, 3, PART, slots), F32),
            pltpu.VMEM((groups, 8, blocks), F32),
            pltpu.VMEM((16, 2, 8, 128), F32),
            pltpu.VMEM((16, 2, 8, 128), F32),
            pltpu.VMEM((groups, 16, 128, 16), F32),
            pltpu.VMEM((4,) + tile, F32),
            pltpu.VMEM((288, 128), BF16),
            pltpu.VMEM((4, 16, 128), F32),
            pltpu.VMEM((192, 128), F32),
            pltpu.VMEM(tile, F32),
            pltpu.VMEM(tile, F32),
            pltpu.VMEM((2,) + tile, F32),
            pltpu.VMEM((2,) + tile, F32),
            pltpu.VMEM((4,) + tile, F32),
            pltpu.VMEM(tile, F32),
            dma((2,)), dma((4,)), dma,
            dma((groups, 16, 2)), dma((groups, 16, 2)), dma((16, 2)), dma((16, 2)),
            dma((4,)), dma((4,)), dma((4,)), dma((4,)), dma((4,)), dma((4,)),
        ],
        compiler_params=pltpu.CompilerParams(
            collective_id=0, has_side_effects=True, vmem_limit_bytes=40 * 2**20
        ),
    )(*(pltpu.with_memory_space_constraint(x, pltpu.HBM) for x in arguments))
    return pl.pallas_call(
        finish,
        out_shape=tuple(jax.ShapeDtypeStruct(x.shape, F32) for x in results),
        in_specs=[vmem, vmem],
        out_specs=(hbm, hbm),
        scratch_shapes=[dma((7,))],
        compiler_params=pltpu.CompilerParams(vmem_limit_bytes=2**20),
    )(*(pltpu.with_memory_space_constraint(x, pltpu.VMEM) for x in results))


def solution(mesh):
    placed = (
        P(None, "ens", ("cx", "cy"), None),
        P("ens", ("cx", "cy")),
        P("ens", ("cx", "cy")),
        P("ens", ("cx", "cy")),
        P(None, "cx", "cy"),
        P(None, "ens", ("cx", "cy"), None),
    )
    return jax.shard_map(
        on_device,
        mesh=mesh,
        in_specs=placed,
        out_specs=(P(None, "ens", ("cx", "cy"), None), P(None, "cx", "cy")),
        check_vma=False,
    )
```

```python
import functools
import math

import jax
import jax.numpy as jnp
from jax import lax
from jax.experimental import pallas as pl
from jax.experimental.pallas import tpu as pltpu
from jax.sharding import PartitionSpec as P

DUMB = 64
NZ = 64
CAP = 48
TIME_STEP = 0.02
WEISSENBERG = 0.5
EXTENSION = 50.0
VISCOSITY = 1.0

PAIRS = ((0, 0), (1, 1), (2, 2), (0, 1), (0, 2), (1, 2))
ALONG_X = (0, 3, 4)
ALONG_Y = (3, 1, 5)
ALONG_Z = (4, 5, 2)

MESH = pl.DeviceIdType.MESH
F32 = jnp.float32
BF16 = jnp.bfloat16

OFFSETS = (
    (2, 2), (2, 1), (1, 2), (2, 3), (3, 2), (2, 0), (0, 2), (1, 1),
    (3, 3), (1, 3), (3, 1), (1, 0), (3, 0), (0, 1), (0, 3),
)
CODE_X = sum(dx * 4**i for i, (dx, _) in enumerate(OFFSETS))
CODE_Z = sum(dz * 4**i for i, (_, dz) in enumerate(OFFSETS))
HALVES = 2
PART = CAP // HALVES
NT = (((1,), (1,)), ((), ()))


def halves_of(values):
    high = values.astype(BF16)
    return high, (values - high.astype(F32)).astype(BF16)


def stencil(field, west, east, south, north):
    row = lax.broadcasted_iota(jnp.int32, field.shape, 0)
    lane = lax.broadcasted_iota(jnp.int32, field.shape, 1)
    rows, width = field.shape
    east_side = jnp.where(row == rows - 1, pltpu.roll(east, rows - 1, 0), pltpu.roll(field, rows - 1, 0))
    west_side = jnp.where(row == 0, pltpu.roll(west, 1, 0), pltpu.roll(field, 1, 0))
    north_side = jnp.where(
        lane >= width - NZ, pltpu.roll(north, width - NZ, 1), pltpu.roll(field, width - NZ, 1)
    )
    south_side = jnp.where(lane < NZ, pltpu.roll(south, NZ, 1), pltpu.roll(field, NZ, 1))
    return east_side, west_side, north_side, south_side


def along_z(field):
    lane = lax.rem(lax.broadcasted_iota(jnp.int32, field.shape, 1), NZ)
    width = field.shape[1]
    upper = jnp.where(lane < NZ - 1, pltpu.roll(field, width - 1, 1), 0.0)
    lower = jnp.where(lane > 0, pltpu.roll(field, 1, 1), 0.0)
    return upper, lower


def kernel(
    conf_hbm, fill_hbm, dest_hbm, cell_hbm, vel_hbm, noise_hbm,
    out_ref, vout_ref,
    conf, fill_ref, dest_ref, cell_ref, vel_ref, noise, terms, sendbuf, recv, labels, labsend, labrecv, columns,
    vhalo, table, rowbuf, field, sx, sy, shx, shy, dv, base,
    conf_sem, in_sem, noise_sem, ssem, rsem, lssem, lrsem, vs_sem, vr_sem, hs_sem, hr_sem, ds_sem, dr_sem,
):
    ens = lax.axis_index("ens")
    cx = lax.axis_index("cx")
    cy = lax.axis_index("cy")
    my_x = lax.div(cx, 2)
    core = lax.rem(cx, 2)
    n_ens = 4

    def conf_copy(g, a):
        return pltpu.make_async_copy(conf_hbm.at[a, g], conf.at[a, g], conf_sem.at[g, a])

    small = [
        pltpu.make_async_copy(source, target, in_sem.at[k])
        for k, (source, target) in enumerate(
            ((dest_hbm, dest_ref), (vel_hbm, vel_ref), (fill_hbm, fill_ref), (cell_hbm, cell_ref))
        )
    ]
    for a in range(3):
        conf_copy(0, a).start()
    for copy in small:
        copy.start()
    noise_copy = pltpu.make_async_copy(noise_hbm, noise, noise_sem)

    east_id = (ens, lax.rem(cx + 1, 8), cy)
    west_id = (ens, lax.rem(cx + 7, 8), cy)
    north_id = (ens, cx, lax.rem(cy + 1, 4))
    south_id = (ens, cx, lax.rem(cy + 3, 4))

    def chip(dx, dz, r):
        return (ens, lax.rem(my_x + dx, 4) * 2 + lax.rem(core + r, 2), lax.rem(cy + dz, 4))

    barrier = pltpu.get_barrier_semaphore()
    for dx, dz in OFFSETS:
        for r in range(2):
            pl.semaphore_signal(barrier, inc=1, device_id=chip(dx, dz, r), device_id_type=MESH)
    pl.semaphore_signal(barrier, inc=1, device_id=chip(0, 0, 1), device_id_type=MESH)
    for k in range(1, n_ens):
        pl.semaphore_signal(
            barrier, inc=1, device_id=(lax.rem(ens + k, n_ens), cx, cy), device_id_type=MESH
        )

    def split(g):
        for a in range(3):
            if g == 0:
                conf_copy(0, a).wait()
                conf_copy(1, a).start()
            first, second = halves_of(conf[a, g])
            terms[g, :, a * 128 : (a + 1) * 128] = first
            terms[g, :, (a + 3) * 128 : (a + 4) * 128] = second

    blocks = conf.shape[2]
    row48 = lax.broadcasted_iota(jnp.int32, (CAP, blocks), 0)
    lane128 = lax.broadcasted_iota(jnp.int32, (1, 128), 1)

    field[...] = jnp.zeros_like(field)
    rowbuf[...] = jnp.zeros_like(rowbuf)
    split(0)
    for copy in small:
        copy.wait()

    def lanes_of(slot):
        return pl.ds(0, 256) if slot < 2 else pl.ds(128, 128) if slot == 2 else pl.ds(0, 128)

    def vel_copy(slot, target):
        return pltpu.make_async_remote_copy(
            src_ref=vel_ref.at[:, :, lanes_of(slot)], dst_ref=vhalo.at[slot, :, :, lanes_of(slot)], send_sem=vs_sem.at[slot], recv_sem=vr_sem.at[slot],
            device_id=target, device_id_type=MESH,
        )

    halo_targets = (east_id, west_id, north_id, south_id)

    def data_copy(g, i, p, r, h, target):
        return pltpu.make_async_remote_copy(
            src_ref=sendbuf.at[g, i, r, h], dst_ref=recv.at[g, p, r, h],
            send_sem=ssem.at[g, i, r], recv_sem=rsem.at[g, p, r],
            device_id=target, device_id_type=MESH,
        )

    def label_copy(p, r, target):
        return pltpu.make_async_remote_copy(
            src_ref=labsend.at[p, r], dst_ref=labrecv.at[p, r],
            send_sem=lssem.at[p, r], recv_sem=lrsem.at[p, r],
            device_id=target, device_id_type=MESH,
        )

    def pack_batch(q, carry, g, width, mode=3):
        code_x, code_z = carry
        targets, landing = [], []
        for _ in range(width):
            dx, dz = lax.rem(code_x, 4), lax.rem(code_z, 4)
            code_x, code_z = lax.div(code_x, 4), lax.div(code_z, 4)
            dx = jnp.where(core == 0, dx, lax.rem(4 - dx, 4))
            dz = jnp.where(core == 0, dz, lax.rem(4 - dz, 4))
            landing.append(dx * 4 + dz)
            targets += [chip(dx, dz, 0), chip(dx, dz, 1)]
        if mode & 1:
            fill_batch(q, g, width, targets)
        if mode & 2:
            start_batch(q, g, width, targets, landing)
        return code_x, code_z

    def fill_batch(q, g, width, targets):
        dest = dest_ref[g : g + 1, :]
        onehot = jnp.concatenate(
            [
                jnp.where(dest - (target[1] * 4 + target[2]) * CAP == row48, 1.0, 0.0).astype(BF16)
                for target in targets
            ],
            axis=0,
        )
        packed = jnp.dot(onehot, terms[g], preferred_element_type=F32)
        packed = packed[:, :384] + packed[:, 384:]
        for n in range(2 * width):
            for h in range(HALVES):
                for a in range(3):
                    sendbuf[g, width * q + n // 2, n % 2, h, a] = packed[
                        n * CAP + h * PART : n * CAP + (h + 1) * PART, a * 128 : (a + 1) * 128
                    ]

    def start_batch(q, g, width, targets, landing):
        def start(first, last):
            for h in range(HALVES):
                for n in range(first, last):
                    data_copy(g, width * q + n // 2, landing[n // 2], n % 2, h, targets[n]).start()

        start(0, 2 * width - 2)

        @pl.when(q < 16 // width - 1)
        def _():
            start(2 * width - 2, 2 * width)

        @pl.when(q == 16 // width - 1)
        def _():
            start(2 * width - 1, 2 * width)
            pltpu.make_async_copy(sendbuf.at[g, 15, 0], recv.at[g, 0, 0], rsem.at[g, 0, 0]).start()

    codes = (jnp.int32(CODE_X), jnp.int32(CODE_Z))

    def send_blocks(g, first, last, width=4, mode=3):
        start = tuple(jnp.int32(code // 4 ** (width * first)) for code in (CODE_X, CODE_Z))
        lax.fori_loop(first, last, functools.partial(pack_batch, g=g, width=width, mode=mode), start)

    send_blocks(0, 0, 2, mode=1)
    pl.semaphore_wait(barrier, 31 + n_ens - 1)
    for slot in range(4):
        vel_copy(slot, halo_targets[slot]).start()
    send_blocks(0, 0, 2, mode=2)

    lab_row = lax.broadcasted_iota(jnp.int32, (8, 128), 0)
    block_lane = lax.broadcasted_iota(jnp.int32, (128, 128), 1)

    def label_rows(k, carry, g):
        rows = pl.ds(pl.multiple_of(k * 128, 128), 128)
        fill = fill_ref[g : g + 1, rows]
        cell = cell_ref[g : g + 1, rows].astype(F32)
        live = block_lane < jnp.broadcast_to(fill, (8, 128)).T[:, 0:1]
        fill = fill.astype(F32)
        x = [jnp.where(live, conf[a, g, rows], 0.0) for a in range(3)]
        inverse = 1.0 / (1.0 - (x[0] * x[0] + x[1] * x[1] + x[2] * x[2]) / EXTENSION)
        spring = [x[a] * inverse for a in range(3)]
        sums = jnp.zeros((128, 128), F32)
        for c, (a, b) in enumerate(PAIRS):
            sums = jnp.where(block_lane == c + 2, jnp.sum(x[a] * spring[b], axis=1, keepdims=True), sums)
        sums = sums.T[:8]
        labels[g, :, rows] = jnp.where(lab_row == 0, fill, jnp.where(lab_row == 1, cell, sums))
        return carry

    for a in range(3):
        conf_copy(1, a).wait()
    noise_copy.start()
    def both_rows(k, carry):
        for g in range(2):
            label_rows(k, carry, g)
        return carry

    lax.fori_loop(0, blocks // 128, both_rows, 0)

    row128 = lax.broadcasted_iota(jnp.int32, (128, blocks), 0)

    def send_labels():
        told = jnp.zeros((256, 128), F32)
        for g in range(2):
            dest = dest_ref[g : g + 1, :]
            owner = ((dest.astype(F32) + 0.5) * (1.0 / CAP)).astype(jnp.int32)
            slot = dest - owner * CAP
            where_to = jnp.where(row128 - 64 * g == slot, 1.0, 0.0).astype(BF16)
            values = labels[g]
            first = values.astype(BF16).astype(F32)
            masks = []
            for p in range(16):
                for r in range(2):
                    _, x, z = chip(p // 4, p % 4, r)
                    masks.append(jnp.broadcast_to(owner == x * 4 + z, values.shape))
            for term in (first, values - first):
                spread = jnp.concatenate(
                    [
                        jnp.concatenate(
                            [jnp.where(masks[n], term, 0.0), jnp.where(masks[n + 1], term, 0.0)], axis=0
                        ).astype(BF16)
                        for n in range(0, 32, 2)
                    ],
                    axis=0,
                )
                told = told + lax.dot_general(spread, where_to, NT, preferred_element_type=F32)
        for p in range(16):
            for r in range(2):
                labsend[p, r] = told[16 * p + 8 * r : 16 * p + 8 * r + 8]
        label_copy(0, 1, chip(0, 0, 1)).start()
        pltpu.make_async_copy(labsend.at[0, 0], labrecv.at[0, 0], lrsem.at[0, 0]).start()

        def start(p, carry):
            for r in range(2):
                label_copy(p, r, chip(lax.div(p, 4), lax.rem(p, 4), r)).start()
            return carry

        lax.fori_loop(1, 16, start, 0)

    send_labels()

    send_blocks(0, 2, 4)
    split(1)
    send_blocks(1, 0, 2)

    for slot in range(4):
        vel_copy(slot, halo_targets[slot]).wait()
    inside = (cx > 0, cx < 7, cy > 0, cy < 3)

    def masked(tile, k):
        return jnp.where(inside[k], tile, 0.0)

    for a in range(3):
        f = vel_ref[a]
        e, w, n, s = stencil(f, *(masked(vhalo[k, a], k) for k in range(4)))
        u, d = along_z(f)
        base[a] = f + TIME_STEP * VISCOSITY * (e + w + n + s + u + d - 6.0 * f)
        for b, slope in enumerate((0.5 * (e - w), 0.5 * (n - s), 0.5 * (u - d))):
            first, second = halves_of(jnp.concatenate([slope[:, :128], slope[:, 128:]], axis=0))
            top = (3 * a + b) * 16
            table[top : top + 16] = first
            table[144 + top : 144 + top + 16] = second

    square = lax.broadcasted_iota(jnp.int32, (128, 128), 0)
    row_hi = lax.broadcasted_iota(jnp.int32, (16, 128), 0)

    def read_labels(q, carry, g):
        told, lows, highs = [], [], []
        for m in range(4):
            p = 4 * q + m
            if g == 0:
                for r in range(2):
                    pltpu.make_async_copy(labrecv.at[p, r], labrecv.at[p, r], lrsem.at[p, r]).wait()
            lab0, lab1 = labrecv[p, 0], labrecv[p, 1]
            if g == 0:
                here = jnp.where(lane128 < 64, lab0, pltpu.roll(lab1, 64, 1))
            else:
                here = jnp.where(lane128 < 64, pltpu.roll(lab0, 64, 1), lab1)
            cells = here[1:2].astype(jnp.int32)
            cell_hi = lax.div(cells, 128)
            cell_hi = lax.rem(cell_hi, 2) * 8 + lax.div(cell_hi, 2)
            told.append(here)
            lows.append(jnp.where(square == lax.rem(cells, 128), 1.0, 0.0).astype(BF16))
            highs.append(jnp.where(row_hi == cell_hi, 1.0, 0.0))
        at_lo = jnp.concatenate(lows, axis=1)
        spread = jnp.concatenate(
            [jnp.concatenate([told[m][c + 2 : c + 3] * highs[m] for c in range(6)], axis=0) for m in range(4)], axis=1
        )
        first, second = halves_of(spread)
        field[...] += lax.dot_general(
            jnp.concatenate([first, second], axis=0), at_lo, NT, preferred_element_type=F32
        )
        looked = jnp.dot(table[...], at_lo, preferred_element_type=F32)
        looked = looked[:144] + looked[144:]
        for m in range(4):
            for c in range(9):
                rowbuf[m, c : c + 1] = jnp.sum(
                    looked[16 * c : 16 * c + 16, 128 * m : 128 * m + 128] * highs[m], axis=0, keepdims=True
                )
            rowbuf[m, 9:10] = told[m][0:1]
        for m in range(4):
            columns[g, 4 * q + m] = rowbuf[m].T
        return carry

    for g in range(2):
        lax.fori_loop(0, 4, functools.partial(read_labels, g=g), 0)

    total = (field[:96] + field[96:]) / (WEISSENBERG * DUMB)
    stress = [
        jnp.concatenate([total[16 * c : 16 * c + 8], total[16 * c + 8 : 16 * c + 16]], axis=1) for c in range(6)
    ]
    for k in range(3):
        sx[k] = stress[ALONG_X[k]]
        sy[k] = stress[ALONG_Y[k]]
        u, d = along_z(stress[ALONG_Z[k]])
        dv[ens, k] = 0.5 * (u - d)

    def stress_copy(slot):
        lanes = lanes_of(slot)
        return pltpu.make_async_remote_copy(
            src_ref=(sx if slot < 2 else sy).at[:, :, lanes],
            dst_ref=(shx.at[slot] if slot < 2 else shy.at[slot - 2]).at[:, :, lanes],
            send_sem=hs_sem.at[slot], recv_sem=hr_sem.at[slot],
            device_id=halo_targets[slot], device_id_type=MESH,
        )

    for slot in range(4):
        stress_copy(slot).start()

    send_blocks(1, 2, 4)
    noise_copy.wait()
    slot_lane = lax.broadcasted_iota(jnp.int32, (CAP, 128), 1).astype(F32)

    def arrive(j, carry, g):
        code_x, code_z = carry
        own = j == 0
        i = lax.rem(j + 15, 16)
        dx = jnp.where(own, 0, lax.rem(code_x, 4))
        dz = jnp.where(own, 0, lax.rem(code_z, 4))
        code_x = jnp.where(own, code_x, lax.div(code_x, 4))
        code_z = jnp.where(own, code_z, lax.div(code_z, 4))
        def sent(r):
            pltpu.make_async_copy(sendbuf.at[g, i, r], sendbuf.at[g, i, r], ssem.at[g, i, r]).wait()
            if g == 0:
                pltpu.make_async_copy(labsend.at[j, r], labsend.at[j, r], lssem.at[j, r]).wait()

        pl.when(j > 0)(lambda: sent(0))
        sent(1)
        for r in range(2):
            landed = recv.at[g, dx * 4 + dz, r]
            pltpu.make_async_copy(landed, landed, rsem.at[g, dx * 4 + dz, r]).wait()
        for r in range(2):
            source = (lax.rem(my_x + 4 - dx, 4) * 2 + lax.rem(core + r, 2)) * 4 + lax.rem(cy + 4 - dz, 4)
            rows = pl.ds(pl.multiple_of(source * CAP, CAP), CAP)
            here = columns[g, dx * 4 + dz, r * 64 : r * 64 + CAP]
            live = slot_lane < here[:, 9:10]
            x = [
                jnp.where(
                    live, jnp.concatenate([recv[g, dx * 4 + dz, r, h, a] for h in range(HALVES)], axis=0), 0.0
                )
                for a in range(3)
            ]
            inverse = 1.0 / (1.0 - (x[0] * x[0] + x[1] * x[1] + x[2] * x[2]) / EXTENSION)
            for a in range(3):
                stretch = sum(here[:, 3 * a + b : 3 * a + b + 1] * x[b] for b in range(3))
                stepped = (
                    x[a]
                    + TIME_STEP * (stretch - x[a] * inverse / (2.0 * WEISSENBERG))
                    + math.sqrt(TIME_STEP / WEISSENBERG) * noise[a, g, rows]
                )
                out_ref[a, g, rows] = jnp.where(live, stepped, 0.0)
        return code_x, code_z

    lax.fori_loop(0, 16, functools.partial(arrive, g=0), codes)
    for slot in range(4):
        stress_copy(slot).wait()
    for k in range(3):
        fx, fy = sx[k], sy[k]
        e, w, _, _ = stencil(fx, masked(shx[0, k], 0), masked(shx[1, k], 1), fx, fx)
        _, _, n, s = stencil(fy, fy, fy, masked(shy[0, k], 2), masked(shy[1, k], 3))
        dv[ens, k] = dv[ens, k] + 0.5 * (e - w) + 0.5 * (n - s)

    def dv_copy(k):
        return pltpu.make_async_remote_copy(
            src_ref=dv.at[ens], dst_ref=dv.at[ens], send_sem=ds_sem.at[k], recv_sem=dr_sem.at[k],
            device_id=(lax.rem(ens + k, n_ens), cx, cy), device_id_type=MESH,
        )

    def dv_arrival(k):
        source = lax.rem(ens + n_ens - k, n_ens)
        pltpu.make_async_copy(dv.at[source], dv.at[source], dr_sem.at[k]).wait()

    for k in range(1, n_ens):
        dv_copy(k).start()


    lax.fori_loop(0, 16, functools.partial(arrive, g=1), codes)

    for k in range(1, n_ens):
        dv_arrival(k)
    vout_ref[...] = base[...] + TIME_STEP * (dv[0] + dv[1] + dv[2] + dv[3])

    for k in range(1, n_ens):
        dv_copy(k).wait_send()


def finish(conf_vmem, velocity_vmem, conf_hbm, velocity_hbm, sems):
    copies = [pltpu.make_async_copy(velocity_vmem, velocity_hbm, sems.at[6])]
    for a in range(3):
        for g in range(2):
            copies.append(pltpu.make_async_copy(conf_vmem.at[a, g], conf_hbm.at[a, g], sems.at[2 * a + g]))
    for copy in copies:
        copy.start()
    for copy in copies:
        copy.wait()


def on_device(conformations, fill_counts, dest_slots, dest_cells, velocity, noise):
    _, groups, blocks, slots = conformations.shape
    vmem = pl.BlockSpec(memory_space=pltpu.VMEM)
    hbm = pl.BlockSpec(memory_space=pl.ANY)
    tile = velocity.shape
    arguments = (conformations, fill_counts, dest_slots, dest_cells, velocity, noise)
    dma = pltpu.SemaphoreType.DMA
    results = pl.pallas_call(
        kernel,
        out_shape=(
            pltpu.VMEM(noise.shape, F32),
            pltpu.VMEM(velocity.shape, F32),
        ),
        in_specs=[hbm] * 6,
        out_specs=(vmem, vmem),
        scratch_shapes=[
            pltpu.VMEM(conformations.shape, F32),
            pltpu.VMEM(fill_counts.shape, jnp.int32),
            pltpu.VMEM(fill_counts.shape, jnp.int32),
            pltpu.VMEM(fill_counts.shape, jnp.int32),
            pltpu.VMEM(tile, F32),
            pltpu.VMEM(noise.shape, F32),
            pltpu.VMEM((groups, blocks, 6 * slots), BF16),
            pltpu.VMEM((groups, 16, 2, HALVES, 3, PART, slots), F32),
            pltpu.VMEM((groups, 16, 2, HALVES, 3, PART, slots), F32),
            pltpu.VMEM((groups, 8, blocks), F32),
            pltpu.VMEM((16, 2, 8, 128), F32),
            pltpu.VMEM((16, 2, 8, 128), F32),
            pltpu.VMEM((groups, 16, 128, 16), F32),
            pltpu.VMEM((4,) + tile, F32),
            pltpu.VMEM((288, 128), BF16),
            pltpu.VMEM((4, 16, 128), F32),
            pltpu.VMEM((192, 128), F32),
            pltpu.VMEM(tile, F32),
            pltpu.VMEM(tile, F32),
            pltpu.VMEM((2,) + tile, F32),
            pltpu.VMEM((2,) + tile, F32),
            pltpu.VMEM((4,) + tile, F32),
            pltpu.VMEM(tile, F32),
            dma((2, 3)), dma((4,)), dma,
            dma((groups, 16, 2)), dma((groups, 16, 2)), dma((16, 2)), dma((16, 2)),
            dma((4,)), dma((4,)), dma((4,)), dma((4,)), dma((4,)), dma((4,)),
        ],
        compiler_params=pltpu.CompilerParams(
            collective_id=0, has_side_effects=True, vmem_limit_bytes=40 * 2**20
        ),
    )(*(pltpu.with_memory_space_constraint(x, pltpu.HBM) for x in arguments))
    return pl.pallas_call(
        finish,
        out_shape=tuple(jax.ShapeDtypeStruct(x.shape, F32) for x in results),
        in_specs=[vmem, vmem],
        out_specs=(hbm, hbm),
        scratch_shapes=[dma((7,))],
        compiler_params=pltpu.CompilerParams(vmem_limit_bytes=2**20),
    )(*(pltpu.with_memory_space_constraint(x, pltpu.VMEM) for x in results))


def solution(mesh):
    placed = (
        P(None, "ens", ("cx", "cy"), None),
        P("ens", ("cx", "cy")),
        P("ens", ("cx", "cy")),
        P("ens", ("cx", "cy")),
        P(None, "cx", "cy"),
        P(None, "ens", ("cx", "cy"), None),
    )
    return jax.shard_map(
        on_device,
        mesh=mesh,
        in_specs=placed,
        out_specs=(P(None, "ens", ("cx", "cy"), None), P(None, "cx", "cy")),
        check_vma=False,
    )
```

```python
import functools
import math

import jax
import jax.numpy as jnp
from jax import lax
from jax.experimental import pallas as pl
from jax.experimental.pallas import tpu as pltpu
from jax.sharding import PartitionSpec as P

DUMB = 64
NZ = 64
CAP = 48
TIME_STEP = 0.02
WEISSENBERG = 0.5
EXTENSION = 50.0
VISCOSITY = 1.0

PAIRS = ((0, 0), (1, 1), (2, 2), (0, 1), (0, 2), (1, 2))
ALONG_X = (0, 3, 4)
ALONG_Y = (3, 1, 5)
ALONG_Z = (4, 5, 2)

MESH = pl.DeviceIdType.MESH
F32 = jnp.float32
BF16 = jnp.bfloat16

OFFSETS = (
    (2, 2), (2, 1), (1, 2), (2, 3), (3, 2), (2, 0), (0, 2), (1, 1),
    (3, 3), (1, 3), (3, 1), (1, 0), (3, 0), (0, 1), (0, 3),
)
CODE_X = sum(dx * 4**i for i, (dx, _) in enumerate(OFFSETS))
CODE_Z = sum(dz * 4**i for i, (_, dz) in enumerate(OFFSETS))
HALVES = 2
PART = CAP // HALVES
NT = (((1,), (1,)), ((), ()))


def halves_of(values):
    high = values.astype(BF16)
    return high, (values - high.astype(F32)).astype(BF16)


def stencil(field, west, east, south, north):
    row = lax.broadcasted_iota(jnp.int32, field.shape, 0)
    lane = lax.broadcasted_iota(jnp.int32, field.shape, 1)
    rows, width = field.shape
    east_side = jnp.where(row == rows - 1, pltpu.roll(east, rows - 1, 0), pltpu.roll(field, rows - 1, 0))
    west_side = jnp.where(row == 0, pltpu.roll(west, 1, 0), pltpu.roll(field, 1, 0))
    north_side = jnp.where(
        lane >= width - NZ, pltpu.roll(north, width - NZ, 1), pltpu.roll(field, width - NZ, 1)
    )
    south_side = jnp.where(lane < NZ, pltpu.roll(south, NZ, 1), pltpu.roll(field, NZ, 1))
    return east_side, west_side, north_side, south_side


def along_z(field):
    lane = lax.rem(lax.broadcasted_iota(jnp.int32, field.shape, 1), NZ)
    width = field.shape[1]
    upper = jnp.where(lane < NZ - 1, pltpu.roll(field, width - 1, 1), 0.0)
    lower = jnp.where(lane > 0, pltpu.roll(field, 1, 1), 0.0)
    return upper, lower


def kernel(
    conf_hbm, fill_hbm, dest_hbm, cell_hbm, vel_hbm, noise_hbm,
    out_ref, vout_ref,
    conf, fill_ref, dest_ref, cell_ref, vel_ref, noise, terms, sendbuf, recv, labels, labsend, labrecv, columns,
    vhalo, table, rowbuf, field, sx, sy, shx, shy, dv, base,
    conf_sem, in_sem, noise_sem, ssem, rsem, lssem, lrsem, vs_sem, vr_sem, hs_sem, hr_sem, ds_sem, dr_sem,
):
    ens = lax.axis_index("ens")
    cx = lax.axis_index("cx")
    cy = lax.axis_index("cy")
    my_x = lax.div(cx, 2)
    core = lax.rem(cx, 2)
    n_ens = 4

    def conf_copy(g, a):
        return pltpu.make_async_copy(conf_hbm.at[a, g], conf.at[a, g], conf_sem.at[g, a])

    small = [
        pltpu.make_async_copy(source, target, in_sem.at[k])
        for k, (source, target) in enumerate(
            ((dest_hbm, dest_ref), (vel_hbm, vel_ref), (fill_hbm, fill_ref), (cell_hbm, cell_ref))
        )
    ]
    for a in range(3):
        conf_copy(0, a).start()
    for copy in small:
        copy.start()
    noise_copy = pltpu.make_async_copy(noise_hbm, noise, noise_sem)

    east_id = (ens, lax.rem(cx + 1, 8), cy)
    west_id = (ens, lax.rem(cx + 7, 8), cy)
    north_id = (ens, cx, lax.rem(cy + 1, 4))
    south_id = (ens, cx, lax.rem(cy + 3, 4))

    def chip(dx, dz, r):
        return (ens, lax.rem(my_x + dx, 4) * 2 + lax.rem(core + r, 2), lax.rem(cy + dz, 4))

    barrier = pltpu.get_barrier_semaphore()
    for dx, dz in OFFSETS:
        for r in range(2):
            pl.semaphore_signal(barrier, inc=1, device_id=chip(dx, dz, r), device_id_type=MESH)
    pl.semaphore_signal(barrier, inc=1, device_id=chip(0, 0, 1), device_id_type=MESH)
    for k in range(1, n_ens):
        pl.semaphore_signal(
            barrier, inc=1, device_id=(lax.rem(ens + k, n_ens), cx, cy), device_id_type=MESH
        )

    def split(g):
        for a in range(3):
            if g == 0:
                conf_copy(0, a).wait()
                conf_copy(1, a).start()
            first, second = halves_of(conf[a, g])
            terms[g, :, a * 128 : (a + 1) * 128] = first
            terms[g, :, (a + 3) * 128 : (a + 4) * 128] = second

    blocks = conf.shape[2]
    row48 = lax.broadcasted_iota(jnp.int32, (CAP, blocks), 0)
    lane128 = lax.broadcasted_iota(jnp.int32, (1, 128), 1)

    field[...] = jnp.zeros_like(field)
    rowbuf[...] = jnp.zeros_like(rowbuf)
    split(0)
    for copy in small:
        copy.wait()

    def vel_copy(slot, target):
        return pltpu.make_async_remote_copy(
            src_ref=vel_ref, dst_ref=vhalo.at[slot], send_sem=vs_sem.at[slot], recv_sem=vr_sem.at[slot],
            device_id=target, device_id_type=MESH,
        )

    halo_targets = (east_id, west_id, north_id, south_id)

    def data_copy(g, i, p, r, h, target):
        return pltpu.make_async_remote_copy(
            src_ref=sendbuf.at[g, i, r, h], dst_ref=recv.at[g, p, r, h],
            send_sem=ssem.at[g, i, r], recv_sem=rsem.at[g, p, r],
            device_id=target, device_id_type=MESH,
        )

    def label_copy(p, r, target):
        return pltpu.make_async_remote_copy(
            src_ref=labsend.at[p, r], dst_ref=labrecv.at[p, r],
            send_sem=lssem.at[p, r], recv_sem=lrsem.at[p, r],
            device_id=target, device_id_type=MESH,
        )

    def pack_batch(q, carry, g, width, mode=3):
        code_x, code_z = carry
        targets, landing = [], []
        for _ in range(width):
            dx, dz = lax.rem(code_x, 4), lax.rem(code_z, 4)
            code_x, code_z = lax.div(code_x, 4), lax.div(code_z, 4)
            dx = jnp.where(core == 0, dx, lax.rem(4 - dx, 4))
            dz = jnp.where(core == 0, dz, lax.rem(4 - dz, 4))
            landing.append(dx * 4 + dz)
            targets += [chip(dx, dz, 0), chip(dx, dz, 1)]
        if mode & 1:
            fill_batch(q, g, width, targets)
        if mode & 2:
            start_batch(q, g, width, targets, landing)
        return code_x, code_z

    def fill_batch(q, g, width, targets):
        dest = dest_ref[g : g + 1, :]
        onehot = jnp.concatenate(
            [
                jnp.where(dest - (target[1] * 4 + target[2]) * CAP == row48, 1.0, 0.0).astype(BF16)
                for target in targets
            ],
            axis=0,
        )
        packed = jnp.dot(onehot, terms[g], preferred_element_type=F32)
        packed = packed[:, :384] + packed[:, 384:]
        for n in range(2 * width):
            for h in range(HALVES):
                for a in range(3):
                    sendbuf[g, width * q + n // 2, n % 2, h, a] = packed[
                        n * CAP + h * PART : n * CAP + (h + 1) * PART, a * 128 : (a + 1) * 128
                    ]

    def start_batch(q, g, width, targets, landing):
        def start(first, last):
            for h in range(HALVES):
                for n in range(first, last):
                    data_copy(g, width * q + n // 2, landing[n // 2], n % 2, h, targets[n]).start()

        start(0, 2 * width - 2)

        @pl.when(q < 16 // width - 1)
        def _():
            start(2 * width - 2, 2 * width)

        @pl.when(q == 16 // width - 1)
        def _():
            start(2 * width - 1, 2 * width)
            pltpu.make_async_copy(sendbuf.at[g, 15, 0], recv.at[g, 0, 0], rsem.at[g, 0, 0]).start()

    codes = (jnp.int32(CODE_X), jnp.int32(CODE_Z))

    def send_blocks(g, first, last, width=4, mode=3):
        start = tuple(jnp.int32(code // 4 ** (width * first)) for code in (CODE_X, CODE_Z))
        lax.fori_loop(first, last, functools.partial(pack_batch, g=g, width=width, mode=mode), start)

    send_blocks(0, 0, 2, mode=1)
    pl.semaphore_wait(barrier, 31 + n_ens - 1)
    for slot in range(4):
        vel_copy(slot, halo_targets[slot]).start()
    send_blocks(0, 0, 2, mode=2)

    lab_row = lax.broadcasted_iota(jnp.int32, (8, 128), 0)
    block_lane = lax.broadcasted_iota(jnp.int32, (128, 128), 1)

    def label_rows(k, carry, g):
        rows = pl.ds(pl.multiple_of(k * 128, 128), 128)
        fill = fill_ref[g : g + 1, rows]
        cell = cell_ref[g : g + 1, rows].astype(F32)
        live = block_lane < jnp.broadcast_to(fill, (8, 128)).T[:, 0:1]
        fill = fill.astype(F32)
        x = [jnp.where(live, conf[a, g, rows], 0.0) for a in range(3)]
        inverse = 1.0 / (1.0 - (x[0] * x[0] + x[1] * x[1] + x[2] * x[2]) / EXTENSION)
        spring = [x[a] * inverse for a in range(3)]
        sums = jnp.zeros((128, 128), F32)
        for c, (a, b) in enumerate(PAIRS):
            sums = jnp.where(block_lane == c + 2, jnp.sum(x[a] * spring[b], axis=1, keepdims=True), sums)
        sums = sums.T[:8]
        labels[g, :, rows] = jnp.where(lab_row == 0, fill, jnp.where(lab_row == 1, cell, sums))
        return carry

    for a in range(3):
        conf_copy(1, a).wait()
    noise_copy.start()
    for g in range(2):
        lax.fori_loop(0, blocks // 128, functools.partial(label_rows, g=g), 0)

    row128 = lax.broadcasted_iota(jnp.int32, (128, blocks), 0)

    def send_labels():
        told = jnp.zeros((256, 128), F32)
        for g in range(2):
            dest = dest_ref[g : g + 1, :]
            owner = ((dest.astype(F32) + 0.5) * (1.0 / CAP)).astype(jnp.int32)
            slot = dest - owner * CAP
            where_to = jnp.where(row128 - 64 * g == slot, 1.0, 0.0).astype(BF16)
            values = labels[g]
            first = values.astype(BF16).astype(F32)
            masks = []
            for p in range(16):
                for r in range(2):
                    _, x, z = chip(p // 4, p % 4, r)
                    masks.append(jnp.broadcast_to(owner == x * 4 + z, values.shape))
            for term in (first, values - first):
                spread = jnp.concatenate(
                    [
                        jnp.concatenate(
                            [jnp.where(masks[n], term, 0.0), jnp.where(masks[n + 1], term, 0.0)], axis=0
                        ).astype(BF16)
                        for n in range(0, 32, 2)
                    ],
                    axis=0,
                )
                told = told + lax.dot_general(spread, where_to, NT, preferred_element_type=F32)
        for p in range(16):
            for r in range(2):
                labsend[p, r] = told[16 * p + 8 * r : 16 * p + 8 * r + 8]
        label_copy(0, 1, chip(0, 0, 1)).start()
        pltpu.make_async_copy(labsend.at[0, 0], labrecv.at[0, 0], lrsem.at[0, 0]).start()

        def start(p, carry):
            for r in range(2):
                label_copy(p, r, chip(lax.div(p, 4), lax.rem(p, 4), r)).start()
            return carry

        lax.fori_loop(1, 16, start, 0)

    send_labels()

    send_blocks(0, 2, 4)
    split(1)
    send_blocks(1, 0, 2)

    for slot in range(4):
        vel_copy(slot, halo_targets[slot]).wait()
    inside = (cx > 0, cx < 7, cy > 0, cy < 3)

    def masked(tile, k):
        return jnp.where(inside[k], tile, 0.0)

    for a in range(3):
        f = vel_ref[a]
        e, w, n, s = stencil(f, *(masked(vhalo[k, a], k) for k in range(4)))
        u, d = along_z(f)
        base[a] = f + TIME_STEP * VISCOSITY * (e + w + n + s + u + d - 6.0 * f)
        for b, slope in enumerate((0.5 * (e - w), 0.5 * (n - s), 0.5 * (u - d))):
            first, second = halves_of(jnp.concatenate([slope[:, :128], slope[:, 128:]], axis=0))
            top = (3 * a + b) * 16
            table[top : top + 16] = first
            table[144 + top : 144 + top + 16] = second

    square = lax.broadcasted_iota(jnp.int32, (128, 128), 0)
    row_hi = lax.broadcasted_iota(jnp.int32, (16, 128), 0)

    def read_labels(q, carry, g):
        told, lows, highs = [], [], []
        for m in range(4):
            p = 4 * q + m
            if g == 0:
                for r in range(2):
                    pltpu.make_async_copy(labrecv.at[p, r], labrecv.at[p, r], lrsem.at[p, r]).wait()
            lab0, lab1 = labrecv[p, 0], labrecv[p, 1]
            if g == 0:
                here = jnp.where(lane128 < 64, lab0, pltpu.roll(lab1, 64, 1))
            else:
                here = jnp.where(lane128 < 64, pltpu.roll(lab0, 64, 1), lab1)
            cells = here[1:2].astype(jnp.int32)
            cell_hi = lax.div(cells, 128)
            cell_hi = lax.rem(cell_hi, 2) * 8 + lax.div(cell_hi, 2)
            told.append(here)
            lows.append(jnp.where(square == lax.rem(cells, 128), 1.0, 0.0).astype(BF16))
            highs.append(jnp.where(row_hi == cell_hi, 1.0, 0.0))
        at_lo = jnp.concatenate(lows, axis=1)
        spread = jnp.concatenate(
            [jnp.concatenate([told[m][c + 2 : c + 3] * highs[m] for c in range(6)], axis=0) for m in range(4)], axis=1
        )
        first, second = halves_of(spread)
        field[...] += lax.dot_general(
            jnp.concatenate([first, second], axis=0), at_lo, NT, preferred_element_type=F32
        )
        looked = jnp.dot(table[...], at_lo, preferred_element_type=F32)
        looked = looked[:144] + looked[144:]
        for m in range(4):
            for c in range(9):
                rowbuf[m, c : c + 1] = jnp.sum(
                    looked[16 * c : 16 * c + 16, 128 * m : 128 * m + 128] * highs[m], axis=0, keepdims=True
                )
            rowbuf[m, 9:10] = told[m][0:1]
        for m in range(4):
            columns[g, 4 * q + m] = rowbuf[m].T
        return carry

    for g in range(2):
        lax.fori_loop(0, 4, functools.partial(read_labels, g=g), 0)

    total = (field[:96] + field[96:]) / (WEISSENBERG * DUMB)
    stress = [
        jnp.concatenate([total[16 * c : 16 * c + 8], total[16 * c + 8 : 16 * c + 16]], axis=1) for c in range(6)
    ]
    for k in range(3):
        sx[k] = stress[ALONG_X[k]]
        sy[k] = stress[ALONG_Y[k]]
        u, d = along_z(stress[ALONG_Z[k]])
        dv[ens, k] = 0.5 * (u - d)

    def stress_copy(slot):
        return pltpu.make_async_remote_copy(
            src_ref=sx if slot < 2 else sy, dst_ref=shx.at[slot] if slot < 2 else shy.at[slot - 2],
            send_sem=hs_sem.at[slot], recv_sem=hr_sem.at[slot],
            device_id=halo_targets[slot], device_id_type=MESH,
        )

    for slot in range(4):
        stress_copy(slot).start()

    send_blocks(1, 2, 4)
    noise_copy.wait()
    slot_lane = lax.broadcasted_iota(jnp.int32, (CAP, 128), 1).astype(F32)

    def arrive(j, carry, g):
        code_x, code_z = carry
        own = j == 0
        i = lax.rem(j + 15, 16)
        dx = jnp.where(own, 0, lax.rem(code_x, 4))
        dz = jnp.where(own, 0, lax.rem(code_z, 4))
        code_x = jnp.where(own, code_x, lax.div(code_x, 4))
        code_z = jnp.where(own, code_z, lax.div(code_z, 4))
        def sent(r):
            pltpu.make_async_copy(sendbuf.at[g, i, r], sendbuf.at[g, i, r], ssem.at[g, i, r]).wait()
            if g == 0:
                pltpu.make_async_copy(labsend.at[j, r], labsend.at[j, r], lssem.at[j, r]).wait()

        pl.when(j > 0)(lambda: sent(0))
        sent(1)
        for r in range(2):
            landed = recv.at[g, dx * 4 + dz, r]
            pltpu.make_async_copy(landed, landed, rsem.at[g, dx * 4 + dz, r]).wait()
        for r in range(2):
            source = (lax.rem(my_x + 4 - dx, 4) * 2 + lax.rem(core + r, 2)) * 4 + lax.rem(cy + 4 - dz, 4)
            rows = pl.ds(pl.multiple_of(source * CAP, CAP), CAP)
            here = columns[g, dx * 4 + dz, r * 64 : r * 64 + CAP]
            live = slot_lane < here[:, 9:10]
            x = [
                jnp.where(
                    live, jnp.concatenate([recv[g, dx * 4 + dz, r, h, a] for h in range(HALVES)], axis=0), 0.0
                )
                for a in range(3)
            ]
            inverse = 1.0 / (1.0 - (x[0] * x[0] + x[1] * x[1] + x[2] * x[2]) / EXTENSION)
            for a in range(3):
                stretch = sum(here[:, 3 * a + b : 3 * a + b + 1] * x[b] for b in range(3))
                stepped = (
                    x[a]
                    + TIME_STEP * (stretch - x[a] * inverse / (2.0 * WEISSENBERG))
                    + math.sqrt(TIME_STEP / WEISSENBERG) * noise[a, g, rows]
                )
                out_ref[a, g, rows] = jnp.where(live, stepped, 0.0)
        return code_x, code_z

    lax.fori_loop(0, 16, functools.partial(arrive, g=0), codes)
    for slot in range(4):
        stress_copy(slot).wait()
    for k in range(3):
        fx, fy = sx[k], sy[k]
        e, w, _, _ = stencil(fx, masked(shx[0, k], 0), masked(shx[1, k], 1), fx, fx)
        _, _, n, s = stencil(fy, fy, fy, masked(shy[0, k], 2), masked(shy[1, k], 3))
        dv[ens, k] = dv[ens, k] + 0.5 * (e - w) + 0.5 * (n - s)

    def dv_copy(k):
        return pltpu.make_async_remote_copy(
            src_ref=dv.at[ens], dst_ref=dv.at[ens], send_sem=ds_sem.at[k], recv_sem=dr_sem.at[k],
            device_id=(lax.rem(ens + k, n_ens), cx, cy), device_id_type=MESH,
        )

    def dv_arrival(k):
        source = lax.rem(ens + n_ens - k, n_ens)
        pltpu.make_async_copy(dv.at[source], dv.at[source], dr_sem.at[k]).wait()

    for k in range(1, n_ens):
        dv_copy(k).start()


    lax.fori_loop(0, 16, functools.partial(arrive, g=1), codes)

    for k in range(1, n_ens):
        dv_arrival(k)
    vout_ref[...] = base[...] + TIME_STEP * (dv[0] + dv[1] + dv[2] + dv[3])

    for k in range(1, n_ens):
        dv_copy(k).wait_send()


def finish(conf_vmem, velocity_vmem, conf_hbm, velocity_hbm, sems):
    copies = [pltpu.make_async_copy(velocity_vmem, velocity_hbm, sems.at[6])]
    for a in range(3):
        for g in range(2):
            copies.append(pltpu.make_async_copy(conf_vmem.at[a, g], conf_hbm.at[a, g], sems.at[2 * a + g]))
    for copy in copies:
        copy.start()
    for copy in copies:
        copy.wait()


def on_device(conformations, fill_counts, dest_slots, dest_cells, velocity, noise):
    _, groups, blocks, slots = conformations.shape
    vmem = pl.BlockSpec(memory_space=pltpu.VMEM)
    hbm = pl.BlockSpec(memory_space=pl.ANY)
    tile = velocity.shape
    arguments = (conformations, fill_counts, dest_slots, dest_cells, velocity, noise)
    dma = pltpu.SemaphoreType.DMA
    results = pl.pallas_call(
        kernel,
        out_shape=(
            pltpu.VMEM(noise.shape, F32),
            pltpu.VMEM(velocity.shape, F32),
        ),
        in_specs=[hbm] * 6,
        out_specs=(vmem, vmem),
        scratch_shapes=[
            pltpu.VMEM(conformations.shape, F32),
            pltpu.VMEM(fill_counts.shape, jnp.int32),
            pltpu.VMEM(fill_counts.shape, jnp.int32),
            pltpu.VMEM(fill_counts.shape, jnp.int32),
            pltpu.VMEM(tile, F32),
            pltpu.VMEM(noise.shape, F32),
            pltpu.VMEM((groups, blocks, 6 * slots), BF16),
            pltpu.VMEM((groups, 16, 2, HALVES, 3, PART, slots), F32),
            pltpu.VMEM((groups, 16, 2, HALVES, 3, PART, slots), F32),
            pltpu.VMEM((groups, 8, blocks), F32),
            pltpu.VMEM((16, 2, 8, 128), F32),
            pltpu.VMEM((16, 2, 8, 128), F32),
            pltpu.VMEM((groups, 16, 128, 16), F32),
            pltpu.VMEM((4,) + tile, F32),
            pltpu.VMEM((288, 128), BF16),
            pltpu.VMEM((4, 16, 128), F32),
            pltpu.VMEM((192, 128), F32),
            pltpu.VMEM(tile, F32),
            pltpu.VMEM(tile, F32),
            pltpu.VMEM((2,) + tile, F32),
            pltpu.VMEM((2,) + tile, F32),
            pltpu.VMEM((4,) + tile, F32),
            pltpu.VMEM(tile, F32),
            dma((2, 3)), dma((4,)), dma,
            dma((groups, 16, 2)), dma((groups, 16, 2)), dma((16, 2)), dma((16, 2)),
            dma((4,)), dma((4,)), dma((4,)), dma((4,)), dma((4,)), dma((4,)),
        ],
        compiler_params=pltpu.CompilerParams(
            collective_id=0, has_side_effects=True, vmem_limit_bytes=40 * 2**20
        ),
    )(*(pltpu.with_memory_space_constraint(x, pltpu.HBM) for x in arguments))
    return pl.pallas_call(
        finish,
        out_shape=tuple(jax.ShapeDtypeStruct(x.shape, F32) for x in results),
        in_specs=[vmem, vmem],
        out_specs=(hbm, hbm),
        scratch_shapes=[dma((7,))],
        compiler_params=pltpu.CompilerParams(vmem_limit_bytes=2**20),
    )(*(pltpu.with_memory_space_constraint(x, pltpu.VMEM) for x in results))


def solution(mesh):
    placed = (
        P(None, "ens", ("cx", "cy"), None),
        P("ens", ("cx", "cy")),
        P("ens", ("cx", "cy")),
        P("ens", ("cx", "cy")),
        P(None, "cx", "cy"),
        P(None, "ens", ("cx", "cy"), None),
    )
    return jax.shard_map(
        on_device,
        mesh=mesh,
        in_specs=placed,
        out_specs=(P(None, "ens", ("cx", "cy"), None), P(None, "cx", "cy")),
        check_vma=False,
    )
```
